128 devices in a mesh: leaf: 64 (over y, z, x), sub: 2 (over core).
Axes of the slice: x: 4, y: 4, z: 4, core: 2. Of those that a mesh axis runs over, the one named last changes fastest.
Arguments:
- multipole: bfloat16 [32768, 256], P(('leaf', 'sub')), may hold values from -6 to 6
- positions: float32 [32768, 3, 128], P(('leaf', 'sub')), may hold values from 0 to 1
- charges: float32 [32768, 128], P(('leaf', 'sub')), may hold values from -0.06 to 0.06
- translate_ops: bfloat16 [64, 256, 256], replicated, may hold values from -0.02734375 to 0.02734375
- upward_ops: bfloat16 [8, 256, 256], replicated, may hold values from -0.015625 to 0.015625
- downward_ops: bfloat16 [8, 256, 256], replicated, may hold values from -0.375 to 0.375
- top_weight: float32 [64, 64], replicated, may hold values from -0.75 to 0.75
- send_cells: int32 [16384, 16], P(('leaf', 'sub')), may hold values from 0 to 255
- send_leaves: int32 [16384, 4], P(('leaf', 'sub')), may hold values from 0 to 255
- list_source: int32 [32768, 189], P(('leaf', 'sub')), may hold values from 0 to 2303, as said below
- list_operator: int32 [32768, 189], P(('leaf', 'sub')), may hold values from 0 to 63
- near_leaves: int32 [32768, 27], P(('leaf', 'sub')), may hold values from 0 to 767, as said below
- move_counts: int32 [128, 2], P(('leaf', 'sub')), may hold values from 0 to 8, as said below
Outputs:
- local_exp: float32 [32768, 256], P(('leaf', 'sub'))
- potential: float32 [32768, 128], P(('leaf', 'sub'))
- arrivals: float32 [2048, 5, 128], P(('leaf', 'sub'))
The draws below stay inside these ranges and needn't reach their ends.
Inputs may be any that keep to these rules, and one draw needn't show every extreme that they name: `list_source`: an entry below 256 is a leaf of the same rank; an entry 256 + e * 16 + s is slot s of the multipoles rank e sends to it. `near_leaves`: an entry below 256 is a leaf of the same rank; an entry 256 + e * 4 + s is slot s of the particle blocks rank e sends to it. move_counts[0, 0] and move_counts[127, 1] are 0, every other entry is 1 or more; each column reaches 8 at some rank.
All inputs are finite; a program needn't handle non-finite values.
Results may differ from the reference program's by a relative error of at most 0.0029.
Values may be sent and summed in bfloat16 or wider, within the bound.
A program may use at most 64 MiB of HBM per device.

```python
import jax
import jax.numpy as jnp
from jax import lax

COEF = 256
LEAF = 128
NOPS = 64
NLIST = 189
NNEAR = 27
CAP = 16
PCAP = 4
MCAP = 8
TOP = 64
CELL_DEV = 256
RANKS = 128
CELLS = 32768


def mixed_index(key, row_count, width, local_count, remote_count):
    choose_key, local_key, remote_key = jax.random.split(key, 3)
    choose = jax.random.randint(choose_key, (row_count, width), 0, 2)
    local_ids = jax.random.randint(local_key, (row_count, width), 0, local_count)
    remote_ids = jax.random.randint(remote_key, (row_count, width), local_count, local_count + remote_count)
    return jnp.where(choose == 1, local_ids, remote_ids).astype(jnp.int32)


def draw_list_source(key, part):
    key = jax.random.fold_in(key, 11)
    return mixed_index(key, CELLS, NLIST, CELL_DEV, RANKS * CAP)


def draw_near_leaves(key, part):
    key = jax.random.fold_in(key, 23)
    return mixed_index(key, CELLS, NNEAR, CELL_DEV, RANKS * PCAP)


def draw_move_counts(key, part):
    key = jax.random.fold_in(key, 37)
    base_key, lower_key, upper_key = jax.random.split(key, 3)
    counts = jax.random.randint(base_key, (RANKS, 2), 1, MCAP // 2 + 1)
    lower_rank = jax.random.randint(lower_key, (), 1, RANKS)
    upper_rank = jax.random.randint(upper_key, (), 0, RANKS - 1)
    rank_ids = jnp.arange(RANKS)
    first_column = jnp.where(rank_ids == lower_rank, MCAP, counts[:, 0])
    second_column = jnp.where(rank_ids == upper_rank, MCAP, counts[:, 1])
    first_column = jnp.where(rank_ids == 0, 0, first_column)
    second_column = jnp.where(rank_ids == RANKS - 1, 0, second_column)
    return jnp.stack([first_column, second_column], 1).astype(jnp.int32)


def with_ends(result, key, least, high):
    shape = result.shape
    spot = [jax.random.randint(jax.random.fold_in(key, axis), (), 0, shape[axis]) for axis in range(len(shape))]
    result = result.at[tuple(spot)].set(least)
    longest = shape.index(max(shape))
    spot[longest] = (spot[longest] + 1) % shape[longest]
    return result.at[tuple(spot)].set(high)


def block_scale(rng, extent, cuts, low, high):
    def one(dim, parts):
        steps = jax.random.uniform(jax.random.fold_in(jax.random.fold_in(rng, 6), dim), (parts,), jnp.float32, low / len(cuts), high / len(cuts))
        return jnp.repeat(jnp.exp(steps), extent[dim] // parts).reshape((-1,) + (1,) * (len(extent) - dim - 1))

    level = one(*cuts[0])
    for cut in cuts[1:]:
        level = level * one(*cut)
    return level


def bell_draw(rng, extent, spread, bound, cuts=(), kind=jnp.bfloat16):
    drawn = spread * jax.random.normal(rng, extent, jnp.float32)
    if cuts:
        drawn = drawn * block_scale(rng, extent, cuts, -0.22, 0.18)
    return jnp.clip(drawn, -bound, bound).astype(kind)


def setup_inputs(seed: int = 0) -> dict:
    key_of = jax.random.split(jax.random.key(seed), 14)
    return {
        "multipole": bell_draw(key_of[0], (CELLS, COEF), 1.0, 6.0, ((0, 128),)),
        "positions": jnp.clip(1.0 * jax.random.uniform(key_of[1], (CELLS, 3, LEAF), jnp.float32) ** block_scale(key_of[1], (CELLS, 3, LEAF), ((0, 128),), -0.2, 0.2), 0.0, 1.0),
        "charges": bell_draw(key_of[2], (CELLS, LEAF), 0.01, 0.06, ((0, 128),), jnp.float32),
        "translate_ops": bell_draw(key_of[3], (NOPS, COEF, COEF), (COEF * NLIST) ** -0.5, 0.02734375),
        "upward_ops": bell_draw(key_of[4], (8, COEF, COEF), (COEF * CELLS // TOP) ** -0.5, 0.015625),
        "downward_ops": bell_draw(key_of[5], (8, COEF, COEF), COEF ** -0.5, 0.375),
        "top_weight": bell_draw(key_of[6], (TOP, TOP), TOP ** -0.5, 0.75, (), jnp.float32),
        "send_cells": with_ends(jax.random.randint(key_of[7], (RANKS * RANKS, CAP), 0, CELL_DEV), jax.random.fold_in(key_of[7], 1), 0, CELL_DEV - 1).astype(jnp.int32),
        "send_leaves": with_ends(jax.random.randint(key_of[8], (RANKS * RANKS, PCAP), 0, CELL_DEV), jax.random.fold_in(key_of[8], 1), 0, CELL_DEV - 1).astype(jnp.int32),
        "list_source": draw_list_source(jax.random.fold_in(key_of[13], 71), 0),
        "list_operator": with_ends(jax.random.randint(key_of[10], (CELLS, NLIST), 0, NOPS), jax.random.fold_in(key_of[10], 1), 0, NOPS - 1).astype(jnp.int32),
        "near_leaves": draw_near_leaves(jax.random.fold_in(key_of[13], 71), 0),
        "move_counts": draw_move_counts(jax.random.fold_in(key_of[13], 71), 0),
    }


SOFTENING = 0.01

def stacked_octants(row_data, first_cell):
    row_count = row_data.shape[0]
    octant = (first_cell + jnp.arange(row_count, dtype=jnp.int32)) % 8
    octant_mask = (octant[:, None] == jnp.arange(8, dtype=jnp.int32)[None, :]).astype(row_data.dtype)
    return (octant_mask[:, :, None] * row_data[:, None, :]).reshape(row_count, 8 * row_data.shape[1])

def near_field(targets, source_pos, source_charge, near_list):

    def one_cell(inputs):
        target, near_ids = inputs
        picked_pos = source_pos[near_ids]
        picked_charge = source_charge[near_ids]
        distance = jnp.zeros((near_ids.shape[0], target.shape[1], target.shape[1]), jnp.float32)
        for axis_id in range(3):
            offset = target[axis_id][None, :, None] - picked_pos[:, axis_id][:, None, :]
            distance = distance + offset * offset
        kernel = lax.rsqrt(distance + SOFTENING)
        return lax.optimization_barrier(jnp.sum(kernel * picked_charge[:, None, :], axis=(0, 2)))
    return lax.map(one_cell, (targets, near_list))

def reference(multipole, positions, charges, translate_ops, upward_ops, downward_ops, top_weight, send_cells, send_leaves, list_source, list_operator, near_leaves, move_counts):
    highest = lax.Precision.HIGHEST
    upward = jnp.dot(stacked_octants(multipole, 0), upward_ops.reshape(8 * COEF, COEF), preferred_element_type=jnp.float32)
    cell_top = jnp.arange(CELLS, dtype=jnp.int32) * TOP // CELLS
    member = (jnp.arange(TOP, dtype=jnp.int32)[:, None] == cell_top[None, :]).astype(jnp.float32)
    top_sums = jnp.dot(member, upward, precision=highest, preferred_element_type=jnp.float32)
    coarse = jnp.dot(top_weight, top_sums, precision=highest, preferred_element_type=jnp.float32).astype(jnp.bfloat16)
    far_top = jnp.dot(stacked_octants(coarse[cell_top], 0), downward_ops.reshape(8 * COEF, COEF), preferred_element_type=jnp.float32)
    sent_cells = send_cells.reshape(RANKS, RANKS, CAP)
    sent_leaves = send_leaves.reshape(RANKS, RANKS, PCAP)
    rank_ids = jnp.arange(RANKS, dtype=jnp.int32)
    ops_flat = translate_ops.reshape(NOPS * COEF, COEF)

    def one_rank(rank_index):
        first_cell = rank_index * CELL_DEV
        own_rows = lax.dynamic_slice_in_dim(multipole, first_cell, CELL_DEV, 0)
        import_rows = (rank_ids[:, None] * CELL_DEV + sent_cells[:, rank_index, :]).reshape(-1)
        source_table = jnp.concatenate([own_rows, multipole[import_rows]], 0)
        source_ids = lax.dynamic_slice_in_dim(list_source, first_cell, CELL_DEV, 0)
        operator_ids = lax.dynamic_slice_in_dim(list_operator, first_cell, CELL_DEV, 0)
        picked = source_table[source_ids].astype(jnp.float32)
        one_hot = (operator_ids[:, :, None] == jnp.arange(NOPS, dtype=jnp.int32)[None, None, :]).astype(jnp.float32)
        grouped = jnp.einsum('cjk,cjf->ckf', one_hot, picked).astype(jnp.bfloat16).reshape(CELL_DEV, NOPS * COEF)
        translated = jnp.dot(grouped, ops_flat, preferred_element_type=jnp.float32)
        leaf_rows = (rank_ids[:, None] * CELL_DEV + sent_leaves[:, rank_index, :]).reshape(-1)
        own_pos = lax.dynamic_slice_in_dim(positions, first_cell, CELL_DEV, 0)
        own_charge = lax.dynamic_slice_in_dim(charges, first_cell, CELL_DEV, 0)
        pos_table = jnp.concatenate([own_pos, positions[leaf_rows]], 0)
        charge_table = jnp.concatenate([own_charge, charges[leaf_rows]], 0)
        near_list = lax.dynamic_slice_in_dim(near_leaves, first_cell, CELL_DEV, 0)
        return (translated, near_field(own_pos, pos_table, charge_table, near_list))
    translated, potential = lax.map(one_rank, rank_ids)
    local_exp = translated.reshape(CELLS, COEF) + far_top
    potential = potential.reshape(CELLS, LEAF)
    payload = jnp.concatenate([positions, charges[:, None, :], potential[:, None, :]], 1)
    slot_index = jnp.arange(MCAP, dtype=jnp.int32)

    def arrivals_of(rank_index):
        upper_rank = jnp.minimum(rank_index + 1, RANKS - 1)
        upper_usable = (rank_index + 1 < RANKS) & (slot_index < move_counts[upper_rank, 0])
        upper_part = jnp.where(upper_usable[:, None, None], payload[upper_rank * CELL_DEV + slot_index], 0.0)
        lower_rank = jnp.maximum(rank_index - 1, 0)
        lower_usable = (rank_index >= 1) & (slot_index < move_counts[lower_rank, 1])
        lower_part = jnp.where(lower_usable[:, None, None], payload[rank_index * CELL_DEV - 1 - slot_index], 0.0)
        return jnp.concatenate([upper_part, lower_part], 0)
    arrivals = lax.map(arrivals_of, rank_ids).reshape(RANKS * 2 * MCAP, 5, LEAF)
    return (local_exp, potential, arrivals)
```

```python
import functools

import jax
import jax.numpy as jnp
from jax import lax
from jax.experimental import pallas as pl
from jax.experimental.pallas import tpu as pltpu
from jax.sharding import PartitionSpec as P

F32 = jnp.float32
BF16 = jnp.bfloat16
MCAP = 8
SOFTENING = 0.01
AXES = ("leaf", "sub")
LANES = 128
FEAT = 32
UNROLL = 8
KSTEP = 8


def shifted(x, axis, by):
    devices = lax.axis_size(axis)
    pairs = [(i, i + by) for i in range(devices) if 0 <= i + by < devices]
    return lax.ppermute(x, axis, pairs)


def pieces(x, count):
    out = []
    for _ in range(count):
        head = x.astype(BF16).astype(F32)
        out.append(head)
        x = x - head
    return out


def main_kernel(
    src_ref,
    near_ref,
    op_ref,
    own_ref,
    got_ref,
    ownp_ref,
    gotp_ref,
    far_ref,
    tr_hbm,
    local_ref,
    pot_ref,
    tab,
    charge,
    target,
    source,
    group_lo,
    group_hi,
    tr_ref,
    tr_sem,
    *picked,
    list_width,
    op_count,
    pitch,
):
    cells = own_ref.shape[0]
    near_count = near_ref.shape[1]
    list_pad = op_ref.shape[1]
    tr_copy = pltpu.make_async_copy(tr_hbm, tr_ref, tr_sem)
    tr_copy.start()
    for buf in picked:
        buf[...] = jnp.zeros_like(buf)

    def spread(ref, base):
        def step(i, carry):
            rows = ref[pl.ds(pl.multiple_of(i * 16, 16), 16), :].astype(F32)
            at = base + i * 32
            tab[pl.ds(at, 16, stride=2), :] = rows[:, :LANES]
            tab[pl.ds(at + 1, 16, stride=2), :] = rows[:, LANES:]
            return carry

        lax.fori_loop(0, ref.shape[0] // 16, step, 0)

    spread(own_ref, 0)
    spread(got_ref, 2 * cells)

    group_lo[...] = jnp.zeros_like(group_lo)
    group_hi[...] = jnp.zeros_like(group_hi)

    def features(ref, first, stage, is_target):
        def step(i, carry):
            at = pl.multiple_of(i * 8, 8)
            axes = [pieces(ref[a, pl.ds(at, 8), :] - 0.5, 2) for a in range(3)]
            norm = jnp.zeros((8, LANES), F32)
            for high, low in axes:
                norm = norm + (high + low) * (high + low)
            one = jnp.ones((8, LANES), F32)
            highs = [a[0] for a in axes]
            lows = [a[1] for a in axes]
            if is_target:
                twice = [-2.0 * h for h in highs], [-2.0 * v for v in lows]
                rows = twice[0] * 2 + twice[1] * 2 + pieces(norm, 3) + [one] * 3
            else:
                rows = (highs + lows) * 2 + [one] * 3 + pieces(norm + SOFTENING, 3)
                charge[pl.ds(first + at, 8), :] = ref[3, pl.ds(at, 8), :]
            for k, row in enumerate(rows):
                stage[pl.ds(at * FEAT + k, 8, stride=FEAT), :] = row
            return carry

        lax.fori_loop(0, ref.shape[1] // 8, step, 0)

    def packed(stage, out, first, count):
        def step(i, carry):
            out[first + i] = stage[pl.ds(pl.multiple_of(i * FEAT, FEAT), FEAT), :].astype(BF16)
            return carry

        lax.fori_loop(0, count, step, 0)

    features(ownp_ref, 0, group_lo, True)
    packed(group_lo, target, 0, cells)
    features(ownp_ref, 0, group_hi, False)
    packed(group_hi, source, 0, cells)
    features(gotp_ref, cells, group_lo, False)
    packed(group_lo, source, cells, gotp_ref.shape[1])

    op_ids = lax.broadcasted_iota(jnp.int32, (op_count, list_pad), 0)

    def group(cell, buf):
        low = buf[pl.ds(0, list_pad, stride=2), :].astype(BF16)
        high = buf[pl.ds(1, list_pad, stride=2), :].astype(BF16)
        hot = jnp.where(op_ids == op_ref[pl.ds(cell, 1), :], 1.0, 0.0).astype(BF16)
        out = jnp.dot(hot, jnp.concatenate([low, high], 1), preferred_element_type=F32)
        group_lo[pl.ds(cell, op_count, stride=pitch), :] = out[:, :LANES]
        group_hi[pl.ds(cell, op_count, stride=pitch), :] = out[:, LANES:]

    def reduced(total, cell):
        pot_ref[pl.ds(cell, 1), :] = jnp.sum(total.T, axis=0, keepdims=True)

    per_pair = -(-list_width // ((near_count + 1) // 2))

    def leaves(c, carry):
        pending = None
        for u in range(UNROLL):
            cell = c * UNROLL + u
            x = target[cell]
            total = jnp.zeros((LANES, LANES), F32)
            taken = 0
            for p in range(0, near_count, 2):
                for j in range(taken, min(taken + per_pair, list_width)):
                    row = pl.multiple_of(src_ref[cell, j], 2)
                    picked[u][2 * j : 2 * j + 2, :] = tab[pl.ds(row, 2), :]
                taken += per_pair
                ids = [near_ref[cell, n] for n in range(p, min(p + 2, near_count))]
                y = [source[i] for i in ids]
                y = jnp.concatenate(y, axis=1) if len(y) > 1 else y[0]
                dist = lax.dot_general(
                    x, y, (((0,), (0,)), ((), ())), preferred_element_type=F32
                )
                for t, i in enumerate(ids):
                    part = lax.rsqrt(dist[:, t * LANES : (t + 1) * LANES])
                    total = total + part * charge[pl.ds(i, 1), :]
                if p == 4:
                    group(jnp.maximum(cell - 1, 0), picked[(u - 1) % UNROLL])
                if p == 8 and pending is not None:
                    reduced(*pending)
            pending = (total, cell)
        reduced(*pending)
        return carry

    lax.fori_loop(0, cells // UNROLL, leaves, 0)
    group(cells - 1, picked[UNROLL - 1])

    tr_copy.wait()
    far = jnp.concatenate([far_ref[...]] * (cells // 8), 0)
    local_ref[...] = far
    width = 2 * LANES

    def translate(k, carry):
        parts = []
        for kk in range(KSTEP):
            at = pl.ds(pl.multiple_of((k * KSTEP + kk) * pitch, 8), cells)
            parts += [group_lo[at, :].astype(BF16), group_hi[at, :].astype(BF16)]
        ops = tr_ref[pl.ds(k * KSTEP, KSTEP)].reshape(KSTEP * width, width)
        local_ref[...] += jnp.dot(
            jnp.concatenate(parts, 1), ops, preferred_element_type=F32
        )
        return carry

    lax.fori_loop(0, op_count // KSTEP, translate, 0)


def main_call(src, near, ops, own, got, own_p, got_p, far, translate_ops):
    cells = own.shape[0]
    list_width = src.shape[1]
    list_pad = ops.shape[1]
    op_count = translate_ops.shape[0]
    tables = cells + got_p.shape[1]
    pitch = cells + 8
    smem = pl.BlockSpec(memory_space=pltpu.SMEM)
    vmem = pl.BlockSpec(memory_space=pltpu.VMEM)
    return pl.pallas_call(
        functools.partial(
            main_kernel, list_width=list_width, op_count=op_count, pitch=pitch
        ),
        out_shape=(
            jax.ShapeDtypeStruct((cells, 2 * LANES), F32),
            jax.ShapeDtypeStruct((cells, LANES), F32),
        ),
        in_specs=[smem, smem] + [vmem] * 6 + [pl.BlockSpec(memory_space=pl.ANY)],
        out_specs=(vmem, vmem),
        scratch_shapes=[
            pltpu.VMEM((2 * (cells + got.shape[0]), LANES), F32),
            pltpu.VMEM((tables, LANES), F32),
            pltpu.VMEM((cells, FEAT, LANES), BF16),
            pltpu.VMEM((tables, FEAT, LANES), BF16),
            pltpu.VMEM((op_count * pitch, LANES), F32),
            pltpu.VMEM((op_count * pitch, LANES), F32),
            pltpu.VMEM(translate_ops.shape, BF16),
            pltpu.SemaphoreType.DMA,
        ]
        + [pltpu.VMEM((2 * list_pad, LANES), F32)] * UNROLL,
        compiler_params=pltpu.CompilerParams(vmem_limit_bytes=60 * 1024 * 1024),
    )(src, near, ops, own, got, own_p, got_p, far, translate_ops)


def per_device(
    multipole,
    positions,
    charges,
    translate_ops,
    upward_ops,
    downward_ops,
    top_weight,
    send_cells,
    send_leaves,
    list_source,
    list_operator,
    near_leaves,
    move_counts,
):
    highest = lax.Precision.HIGHEST
    cells, width = multipole.shape
    leaf_size = positions.shape[2]
    ranks = lax.axis_size(AXES)
    rank = lax.axis_index(AXES)
    tops = top_weight.shape[0]

    octants = jnp.sum(multipole.astype(F32).reshape(cells // 8, 8, width), axis=0)
    share = jnp.dot(
        octants.reshape(1, 8 * width),
        upward_ops.astype(F32).reshape(8 * width, width),
        precision=highest,
        preferred_element_type=F32,
    )

    body = jnp.concatenate([positions, charges[:, None, :]], 1)
    sent = body[send_leaves].reshape(ranks, -1, leaf_size)
    share_rows = jnp.broadcast_to(share.reshape(1, 2, leaf_size), (ranks, 2, leaf_size))
    sent = jnp.concatenate([sent, share_rows], 1)
    got = lax.all_to_all(sent, AXES, split_axis=0, concat_axis=0, tiled=True)

    pick = (send_cells.reshape(-1, 1) == jnp.arange(cells, dtype=jnp.int32)[None, :])
    out_cells = jnp.dot(pick.astype(BF16), multipole, preferred_element_type=F32)
    out_cells = out_cells.astype(BF16).reshape(ranks, -1, width)
    got_cells = lax.all_to_all(out_cells, AXES, split_axis=0, concat_axis=0, tiled=True)

    shares = got[:, -2:, :].reshape(tops, ranks // tops, width)
    top_sums = jnp.sum(shares, axis=1)
    top = rank * tops // ranks
    weight = lax.dynamic_slice_in_dim(top_weight, top, 1, 0)
    coarse = jnp.dot(weight, top_sums, precision=highest, preferred_element_type=F32)
    coarse = jnp.broadcast_to(coarse.astype(BF16)[None], (8, 1, width))
    far = lax.dot_general(
        coarse, downward_ops, (((2,), (1,)), ((0,), (0,))), preferred_element_type=F32
    ).reshape(8, width)

    own_p = jnp.transpose(body, (1, 0, 2))
    got_p = got[:, :-2, :].reshape(-1, 4, leaf_size)
    got_p = jnp.transpose(got_p, (1, 0, 2))
    list_pad = -(-list_operator.shape[1] // 64) * 64
    ops = jnp.pad(
        list_operator,
        ((0, 0), (0, list_pad - list_operator.shape[1])),
        constant_values=translate_ops.shape[0],
    )
    local_exp, potential = main_call(
        list_source * 2,
        near_leaves,
        ops,
        multipole,
        got_cells.reshape(-1, width),
        own_p,
        got_p,
        far,
        translate_ops,
    )

    def payload(a, b):
        return jnp.concatenate([body[a:b], potential[a:b, None, :]], 1)

    slot = jnp.arange(MCAP, dtype=jnp.int32)
    lower = jnp.where((slot < move_counts[0, 0])[:, None, None], payload(0, MCAP), 0.0)
    upper = payload(cells - MCAP, cells)[::-1]
    upper = jnp.where((slot < move_counts[0, 1])[:, None, None], upper, 0.0)
    from_upper = shifted(lower, AXES, -1)
    from_lower = shifted(upper, AXES, 1)
    arrivals = jnp.concatenate([from_upper, from_lower], 0)
    return (local_exp, potential, arrivals)


def solution(mesh):
    rows = P(AXES, None)
    blocks = P(AXES, None, None)
    placed = (rows, blocks, rows) + (P(),) * 4 + (rows,) * 6
    return jax.shard_map(
        per_device,
        mesh=mesh,
        in_specs=placed,
        out_specs=(rows, rows, blocks),
        check_vma=False,
    )
```

```python
import functools

import jax
import jax.numpy as jnp
from jax import lax
from jax.experimental import pallas as pl
from jax.experimental.pallas import tpu as pltpu
from jax.sharding import PartitionSpec as P

F32 = jnp.float32
BF16 = jnp.bfloat16
MCAP = 8
SOFTENING = 0.01
AXES = ("leaf", "sub")
LANES = 128
FEAT = 32
UNROLL = 8
KSTEP = 8


def shifted(x, axis, by):
    devices = lax.axis_size(axis)
    pairs = [(i, i + by) for i in range(devices) if 0 <= i + by < devices]
    return lax.ppermute(x, axis, pairs)


def pieces(x, count):
    out = []
    for _ in range(count):
        head = x.astype(BF16).astype(F32)
        out.append(head)
        x = x - head
    return out


def partner(rank):
    subs = lax.axis_size("sub")
    return (rank // subs, lax.rem(rank, subs))


def halves_in_rows(ref, out, base):
    def step(i, carry):
        rows = ref[pl.ds(pl.multiple_of(i * 16, 16), 16), :].astype(F32)
        at = base + i * 32
        out[pl.ds(at, 16, stride=2), :] = rows[:, :LANES]
        out[pl.ds(at + 1, 16, stride=2), :] = rows[:, LANES:]
        return carry

    lax.fori_loop(0, ref.shape[0] // 16, step, 0, unroll=4)


def pack_kernel(
    cell_ids, leaf_ids, own_ref, body_ref, up_ref, out_cells, out_body, share, tab, stage
):
    ranks, cap, width = out_cells.shape
    blocks = out_body.shape[1] // 4
    halves_in_rows(own_ref, tab, 0)

    def pick(r, carry):
        for s in range(cap):
            row = pl.multiple_of(cell_ids[r * cap + s], 2)
            stage[pl.ds(r * 2 * cap + 2 * s, 2), :] = tab[pl.ds(row, 2), :]
        for s in range(blocks):
            row = pl.multiple_of(leaf_ids[r * blocks + s], 4)
            out_body[r, 4 * s : 4 * s + 4, :] = body_ref[pl.ds(row, 4), :]
        return carry

    lax.fori_loop(0, ranks, pick, 0, unroll=2)

    def pack(r, carry):
        low = stage[pl.ds(r * 2 * cap, cap, stride=2), :]
        high = stage[pl.ds(r * 2 * cap + 1, cap, stride=2), :]
        out_cells[r] = jnp.concatenate([low, high], 1).astype(BF16)
        return carry

    lax.fori_loop(0, ranks, pack, 0, unroll=4)

    rows = own_ref.shape[0]
    octants = jnp.sum(own_ref[...].astype(F32).reshape(rows // 8, 8, width), axis=0)
    lhs = jnp.concatenate(pieces(octants, 3) + [jnp.zeros((8, width), F32)], 0)
    lhs = lhs.astype(BF16)
    row_octant = lax.rem(lax.broadcasted_iota(jnp.int32, (32, width), 0), 8)

    def lift(o, total):
        out = jnp.dot(lhs, up_ref[o], preferred_element_type=F32)
        return total + jnp.where(row_octant == o, out, 0.0)

    lifted = lax.fori_loop(0, 8, lift, jnp.zeros((32, width), F32), unroll=True)
    lifted = jnp.sum(lifted, axis=0, keepdims=True)
    share[0:1, :] = lifted[:, :LANES]
    share[1:2, :] = lifted[:, LANES:]


def pack(cell_ids, leaf_ids, own, body, upward_ops, ranks):
    width = own.shape[1]
    cap = cell_ids.shape[0] // ranks
    rows = 4 * (leaf_ids.shape[0] // ranks)
    smem = pl.BlockSpec(memory_space=pltpu.SMEM)
    vmem = pl.BlockSpec(memory_space=pltpu.VMEM)
    return pl.pallas_call(
        pack_kernel,
        out_shape=(
            jax.ShapeDtypeStruct((ranks, cap, width), BF16),
            jax.ShapeDtypeStruct((ranks, rows, LANES), F32),
            jax.ShapeDtypeStruct((2, LANES), F32),
        ),
        in_specs=[smem] * 2 + [vmem] * 3,
        out_specs=(vmem,) * 3,
        scratch_shapes=[
            pltpu.VMEM((2 * own.shape[0], LANES), F32),
            pltpu.VMEM((ranks * 2 * cap, LANES), F32),
        ],
        compiler_params=pltpu.CompilerParams(vmem_limit_bytes=32 * 1024 * 1024),
    )(cell_ids, leaf_ids, own, body, upward_ops)


def exchange_kernel(
    weight_ref,
    share,
    down_ref,
    out_cells,
    out_body,
    got_cells,
    got_body,
    far_ref,
    shares,
    send_sems,
    recv_sems,
    local_sems,
):
    me = lax.axis_index(AXES)
    ranks = shares.shape[0]
    tops = ranks // 2
    width = 2 * LANES
    barrier = pltpu.get_barrier_semaphore()

    def greet(d, carry):
        pl.semaphore_signal(
            barrier,
            inc=1,
            device_id=partner(lax.rem(me + d, ranks)),
            device_id_type=pl.DeviceIdType.MESH,
        )
        return carry

    lax.fori_loop(1, ranks, greet, 0)
    keep = [
        pltpu.make_async_copy(out_cells.at[me], got_cells.at[me], local_sems.at[0]),
        pltpu.make_async_copy(out_body.at[me], got_body.at[me], local_sems.at[1]),
    ]
    for copy in keep:
        copy.start()
    shares[me] = share[...]
    pl.semaphore_wait(barrier, ranks - 1)

    def remote(src, dst, k, r):
        return pltpu.make_async_remote_copy(
            src_ref=src,
            dst_ref=dst,
            send_sem=send_sems.at[k],
            recv_sem=recv_sems.at[k],
            device_id=partner(r),
            device_id_type=pl.DeviceIdType.MESH,
        )

    def send(d, carry):
        r = lax.rem(me + d, ranks)
        remote(share, shares.at[me], 2, r).start()
        remote(out_cells.at[r], got_cells.at[me], 0, r).start()
        remote(out_body.at[r], got_body.at[me], 1, r).start()
        return carry

    lax.fori_loop(1, ranks, send, 0)

    whole = pl.ds(0, ranks - 1)
    later = lax.rem(me + 1, ranks)
    remote(shares.at[whole], shares.at[whole], 2, later).wait_recv()

    top = me // 2

    def weigh(t, total):
        pair = shares[2 * t] + shares[2 * t + 1]
        return total + weight_ref[top * tops + t] * pair

    coarse = lax.fori_loop(0, tops, weigh, jnp.zeros((2, LANES), F32))
    coarse = jnp.concatenate([coarse[0:1, :], coarse[1:2, :]], 1)
    coarse = jnp.broadcast_to(coarse, (16, width)).astype(BF16)
    for o in range(8):
        out = jnp.dot(coarse, down_ref[o], preferred_element_type=F32)
        far_ref[o : o + 1, :] = out[0:1, :]

    for copy in keep:
        copy.wait()
    remote(shares.at[whole], shares.at[whole], 2, later).wait_send()
    remote(out_cells.at[whole], got_cells.at[whole], 0, later).wait()
    remote(out_body.at[whole], got_body.at[whole], 1, later).wait()


def exchange(weight, share, downward_ops, out_cells, out_body):
    ranks, _, width = out_cells.shape
    smem = pl.BlockSpec(memory_space=pltpu.SMEM)
    vmem = pl.BlockSpec(memory_space=pltpu.VMEM)
    hbm = pl.BlockSpec(memory_space=pl.ANY)
    return pl.pallas_call(
        exchange_kernel,
        out_shape=(
            jax.ShapeDtypeStruct(out_cells.shape, BF16),
            jax.ShapeDtypeStruct(out_body.shape, F32),
            jax.ShapeDtypeStruct((8, width), F32),
        ),
        in_specs=[smem, vmem, vmem, hbm, hbm],
        out_specs=(hbm, hbm, vmem),
        scratch_shapes=[
            pltpu.VMEM((ranks, 2, LANES), F32),
            pltpu.SemaphoreType.DMA((3,)),
            pltpu.SemaphoreType.DMA((3,)),
            pltpu.SemaphoreType.DMA((2,)),
        ],
        compiler_params=pltpu.CompilerParams(
            collective_id=0,
            has_side_effects=True,
            vmem_limit_bytes=32 * 1024 * 1024,
        ),
    )(weight, share, downward_ops, out_cells, out_body)


def main_kernel(
    src_hbm,
    near_hbm,
    op_ref,
    own_ref,
    got_ref,
    ownp_ref,
    gotp_ref,
    far_ref,
    tr_hbm,
    local_ref,
    pot_ref,
    tab,
    charge,
    target,
    source,
    group_lo,
    group_hi,
    tr_ref,
    src_ref,
    near_ref,
    sems,
    *picked,
    list_width,
    op_count,
    pitch,
):
    cells = own_ref.shape[0]
    near_count = near_hbm.shape[0] // cells
    list_pad = op_ref.shape[1]
    src_copy = pltpu.make_async_copy(src_hbm, src_ref, sems.at[0])
    near_copy = pltpu.make_async_copy(near_hbm, near_ref, sems.at[1])
    tr_copy = pltpu.make_async_copy(tr_hbm, tr_ref, sems.at[2])
    near_copy.start()
    src_copy.start()
    tr_copy.start()
    for buf in picked:
        buf[...] = jnp.zeros_like(buf)

    halves_in_rows(own_ref, tab, 0)
    halves_in_rows(got_ref, tab, 2 * cells)

    group_lo[...] = jnp.zeros_like(group_lo)
    group_hi[...] = jnp.zeros_like(group_hi)

    def features(ref, first, stage, is_target):
        def step(i, carry):
            at = pl.multiple_of(i * 8, 8)
            block = [ref[pl.ds(at * 4 + a, 8, stride=4), :] for a in range(4)]
            axes = [pieces(b - 0.5, 2) for b in block[:3]]
            norm = jnp.zeros((8, LANES), F32)
            for high, low in axes:
                norm = norm + (high + low) * (high + low)
            one = jnp.ones((8, LANES), F32)
            highs = [a[0] for a in axes]
            lows = [a[1] for a in axes]
            if is_target:
                twice = [-2.0 * h for h in highs], [-2.0 * v for v in lows]
                rows = twice[0] * 2 + twice[1] * 2 + pieces(norm, 3) + [one] * 3
            else:
                rows = (highs + lows) * 2 + [one] * 3 + pieces(norm + SOFTENING, 3)
                charge[pl.ds(first + at, 8), :] = block[3]
            for k, row in enumerate(rows):
                stage[pl.ds(at * FEAT + k, 8, stride=FEAT), :] = row
            return carry

        lax.fori_loop(0, ref.shape[0] // 32, step, 0, unroll=4)

    def packed(stage, out, first, count):
        def step(i, carry):
            out[first + i] = stage[pl.ds(pl.multiple_of(i * FEAT, FEAT), FEAT), :].astype(BF16)
            return carry

        lax.fori_loop(0, count, step, 0, unroll=8)

    features(ownp_ref, 0, group_lo, True)
    packed(group_lo, target, 0, cells)
    features(ownp_ref, 0, group_hi, False)
    packed(group_hi, source, 0, cells)
    features(gotp_ref, cells, group_lo, False)
    packed(group_lo, source, cells, gotp_ref.shape[0] // 4)

    near_copy.wait()
    src_copy.wait()
    op_ids = lax.broadcasted_iota(jnp.int32, (op_count, list_pad), 0)

    def group(cell, buf):
        low = buf[pl.ds(0, list_pad, stride=2), :].astype(BF16)
        high = buf[pl.ds(1, list_pad, stride=2), :].astype(BF16)
        hot = jnp.where(op_ids == op_ref[pl.ds(cell, 1), :], 1.0, 0.0).astype(BF16)
        out = jnp.dot(hot, jnp.concatenate([low, high], 1), preferred_element_type=F32)
        group_lo[pl.ds(cell, op_count, stride=pitch), :] = out[:, :LANES]
        group_hi[pl.ds(cell, op_count, stride=pitch), :] = out[:, LANES:]

    def reduced(total, cell):
        pot_ref[pl.ds(cell, 1), :] = jnp.sum(total.T, axis=0, keepdims=True)

    per_pair = -(-list_width // ((near_count + 1) // 2))

    def leaves(c, carry):
        pending = None
        for u in range(UNROLL):
            cell = c * UNROLL + u
            x = target[cell]
            src_at = cell * list_width
            near_at = cell * near_count
            total = jnp.zeros((LANES, LANES), F32)
            taken = 0
            for p in range(0, near_count, 2):
                for j in range(taken, min(taken + per_pair, list_width)):
                    row = pl.multiple_of(src_ref[src_at + j], 2)
                    picked[u][2 * j : 2 * j + 2, :] = tab[pl.ds(row, 2), :]
                taken += per_pair
                ids = [near_ref[near_at + n] for n in range(p, min(p + 2, near_count))]
                y = [source[i] for i in ids]
                y = jnp.concatenate(y, axis=1) if len(y) > 1 else y[0]
                dist = lax.dot_general(
                    x, y, (((0,), (0,)), ((), ())), preferred_element_type=F32
                )
                for t, i in enumerate(ids):
                    part = lax.rsqrt(dist[:, t * LANES : (t + 1) * LANES])
                    total = total + part * charge[pl.ds(i, 1), :]
                if p == 4:
                    group(jnp.maximum(cell - 1, 0), picked[(u - 1) % UNROLL])
                if p == 8 and pending is not None:
                    reduced(*pending)
            pending = (total, cell)
        reduced(*pending)
        return carry

    lax.fori_loop(0, cells // UNROLL, leaves, 0)
    group(cells - 1, picked[UNROLL - 1])

    tr_copy.wait()
    far = jnp.concatenate([far_ref[...]] * (cells // 8), 0)
    local_ref[...] = far
    width = 2 * LANES

    def translate(k, carry):
        parts = []
        for kk in range(KSTEP):
            at = pl.ds(pl.multiple_of((k * KSTEP + kk) * pitch, 8), cells)
            parts += [group_lo[at, :].astype(BF16), group_hi[at, :].astype(BF16)]
        ops = tr_ref[pl.ds(k * KSTEP, KSTEP)].reshape(KSTEP * width, width)
        local_ref[...] += jnp.dot(
            jnp.concatenate(parts, 1), ops, preferred_element_type=F32
        )
        return carry

    lax.fori_loop(0, op_count // KSTEP, translate, 0)


def main_call(src, near, ops, own, got, own_p, got_p, far, translate_ops):
    cells = own.shape[0]
    list_width = src.shape[0] // cells
    list_pad = ops.shape[1]
    op_count = translate_ops.shape[0]
    tables = cells + got_p.shape[0] // 4
    pitch = cells + 8
    hbm = pl.BlockSpec(memory_space=pl.ANY)
    vmem = pl.BlockSpec(memory_space=pltpu.VMEM)
    return pl.pallas_call(
        functools.partial(
            main_kernel, list_width=list_width, op_count=op_count, pitch=pitch
        ),
        out_shape=(
            jax.ShapeDtypeStruct((cells, 2 * LANES), F32),
            jax.ShapeDtypeStruct((cells, LANES), F32),
        ),
        in_specs=[hbm, hbm] + [vmem] * 6 + [hbm],
        out_specs=(vmem, vmem),
        scratch_shapes=[
            pltpu.VMEM((2 * (cells + got.shape[0]), LANES), F32),
            pltpu.VMEM((tables, LANES), F32),
            pltpu.VMEM((cells, FEAT, LANES), BF16),
            pltpu.VMEM((tables, FEAT, LANES), BF16),
            pltpu.VMEM((op_count * pitch, LANES), F32),
            pltpu.VMEM((op_count * pitch, LANES), F32),
            pltpu.VMEM(translate_ops.shape, BF16),
            pltpu.SMEM(src.shape, jnp.int32),
            pltpu.SMEM(near.shape, jnp.int32),
            pltpu.SemaphoreType.DMA((3,)),
        ]
        + [pltpu.VMEM((2 * list_pad, LANES), F32)] * UNROLL,
        compiler_params=pltpu.CompilerParams(vmem_limit_bytes=60 * 1024 * 1024),
    )(src, near, ops, own, got, own_p, got_p, far, translate_ops)


def per_device(
    multipole,
    positions,
    charges,
    translate_ops,
    upward_ops,
    downward_ops,
    top_weight,
    send_cells,
    send_leaves,
    list_source,
    list_operator,
    near_leaves,
    move_counts,
):
    cells, width = multipole.shape
    leaf_size = positions.shape[2]
    ranks = lax.axis_size(AXES)

    body = jnp.concatenate([positions, charges[:, None, :]], 1)
    flat = body.reshape(-1, leaf_size)
    out_cells, out_body, share = pack(
        (send_cells * 2).reshape(-1),
        (send_leaves * 4).reshape(-1),
        multipole,
        flat,
        upward_ops,
        ranks,
    )
    got_cells, got_body, far = exchange(
        top_weight.reshape(-1), share, downward_ops, out_cells, out_body
    )
    list_pad = -(-list_operator.shape[1] // 64) * 64
    ops = jnp.pad(
        list_operator,
        ((0, 0), (0, list_pad - list_operator.shape[1])),
        constant_values=translate_ops.shape[0],
    )
    local_exp, potential = main_call(
        (list_source * 2).reshape(-1),
        near_leaves.reshape(-1),
        ops,
        multipole,
        got_cells.reshape(-1, width),
        flat,
        got_body.reshape(-1, leaf_size),
        far,
        translate_ops,
    )

    def payload(a, b):
        return jnp.concatenate([body[a:b], potential[a:b, None, :]], 1)

    slot = jnp.arange(MCAP, dtype=jnp.int32)
    lower = jnp.where((slot < move_counts[0, 0])[:, None, None], payload(0, MCAP), 0.0)
    upper = payload(cells - MCAP, cells)[::-1]
    upper = jnp.where((slot < move_counts[0, 1])[:, None, None], upper, 0.0)
    from_upper = shifted(lower, AXES, -1)
    from_lower = shifted(upper, AXES, 1)
    arrivals = jnp.concatenate([from_upper, from_lower], 0)
    return (local_exp, potential, arrivals)


def solution(mesh):
    rows = P(AXES, None)
    blocks = P(AXES, None, None)
    placed = (rows, blocks, rows) + (P(),) * 4 + (rows,) * 6
    return jax.shard_map(
        per_device,
        mesh=mesh,
        in_specs=placed,
        out_specs=(rows, rows, blocks),
        check_vma=False,
    )
```

```python
import functools

import jax
import jax.numpy as jnp
from jax import lax
from jax.experimental import pallas as pl
from jax.experimental.pallas import tpu as pltpu
from jax.sharding import PartitionSpec as P

F32 = jnp.float32
BF16 = jnp.bfloat16
MCAP = 8
SOFTENING = 0.01
AXES = ("leaf", "sub")
LANES = 128
FEAT = 32
UNROLL = 16
KSTEP = 8
SPREAD = 45


def shifted(x, axis, by):
    devices = lax.axis_size(axis)
    pairs = [(i, i + by) for i in range(devices) if 0 <= i + by < devices]
    return lax.ppermute(x, axis, pairs)


def pieces(x, count):
    out = []
    for _ in range(count):
        head = x.astype(BF16).astype(F32)
        out.append(head)
        x = x - head
    return out


def partner(rank):
    subs = lax.axis_size("sub")
    return (rank // subs, lax.rem(rank, subs))


def halves_in_rows(ref, out, base):
    def step(i, carry):
        rows = ref[pl.ds(pl.multiple_of(i * 16, 16), 16), :].astype(F32)
        at = base + i * 32
        out[pl.ds(at, 16, stride=2), :] = rows[:, :LANES]
        out[pl.ds(at + 1, 16, stride=2), :] = rows[:, LANES:]
        return carry

    lax.fori_loop(0, ref.shape[0] // 16, step, 0, unroll=4)


def pack_kernel(
    cell_ids, leaf_ids, own_ref, body_ref, up_ref, out_cells, out_body, share, tab, stage
):
    ranks, cap, width = out_cells.shape
    blocks = out_body.shape[1] // 4
    halves_in_rows(own_ref, tab, 0)

    def pick(r, carry):
        for s in range(cap):
            row = pl.multiple_of(cell_ids[r * cap + s], 2)
            stage[pl.ds(r * 2 * cap + 2 * s, 2), :] = tab[pl.ds(row, 2), :]
        for s in range(blocks):
            row = pl.multiple_of(leaf_ids[r * blocks + s], 4)
            out_body[r, 4 * s : 4 * s + 4, :] = body_ref[pl.ds(row, 4), :]
        return carry

    lax.fori_loop(0, ranks, pick, 0, unroll=2)

    def pack(r, carry):
        low = stage[pl.ds(r * 2 * cap, cap, stride=2), :]
        high = stage[pl.ds(r * 2 * cap + 1, cap, stride=2), :]
        out_cells[r] = jnp.concatenate([low, high], 1).astype(BF16)
        return carry

    lax.fori_loop(0, ranks, pack, 0, unroll=4)

    rows = own_ref.shape[0]
    octants = jnp.sum(own_ref[...].astype(F32).reshape(rows // 8, 8, width), axis=0)
    lhs = jnp.concatenate(pieces(octants, 3) + [jnp.zeros((8, width), F32)], 0)
    lhs = lhs.astype(BF16)
    row_octant = lax.rem(lax.broadcasted_iota(jnp.int32, (32, width), 0), 8)

    def lift(o, total):
        out = jnp.dot(lhs, up_ref[o], preferred_element_type=F32)
        return total + jnp.where(row_octant == o, out, 0.0)

    lifted = lax.fori_loop(0, 8, lift, jnp.zeros((32, width), F32), unroll=True)
    lifted = jnp.sum(lifted, axis=0, keepdims=True)
    share[0:1, :] = lifted[:, :LANES]
    share[1:2, :] = lifted[:, LANES:]


def pack(cell_ids, leaf_ids, own, body, upward_ops, ranks):
    width = own.shape[1]
    cap = cell_ids.shape[0] // ranks
    rows = 4 * (leaf_ids.shape[0] // ranks)
    smem = pl.BlockSpec(memory_space=pltpu.SMEM)
    vmem = pl.BlockSpec(memory_space=pltpu.VMEM)
    return pl.pallas_call(
        pack_kernel,
        out_shape=(
            jax.ShapeDtypeStruct((ranks, cap, width), BF16),
            jax.ShapeDtypeStruct((ranks, rows, LANES), F32),
            jax.ShapeDtypeStruct((2, LANES), F32),
        ),
        in_specs=[smem] * 2 + [vmem] * 3,
        out_specs=(vmem,) * 3,
        scratch_shapes=[
            pltpu.VMEM((2 * own.shape[0], LANES), F32),
            pltpu.VMEM((ranks * 2 * cap, LANES), F32),
        ],
        compiler_params=pltpu.CompilerParams(vmem_limit_bytes=32 * 1024 * 1024),
    )(cell_ids, leaf_ids, own, body, upward_ops)


def exchange_kernel(
    weight_ref,
    share,
    down_ref,
    out_cells,
    out_body,
    got_cells,
    got_body,
    far_ref,
    shares,
    send_sems,
    recv_sems,
    local_sems,
):
    me = lax.axis_index(AXES)
    ranks = shares.shape[0]
    tops = ranks // 2
    width = 2 * LANES
    barrier = pltpu.get_barrier_semaphore()

    def greet(d, carry):
        pl.semaphore_signal(
            barrier,
            inc=1,
            device_id=partner(lax.rem(me + d, ranks)),
            device_id_type=pl.DeviceIdType.MESH,
        )
        return carry

    lax.fori_loop(1, ranks, greet, 0)
    keep = [
        pltpu.make_async_copy(out_cells.at[me], got_cells.at[me], local_sems.at[0]),
        pltpu.make_async_copy(out_body.at[me], got_body.at[me], local_sems.at[1]),
    ]
    for copy in keep:
        copy.start()
    shares[me] = share[...]
    pl.semaphore_wait(barrier, ranks - 1)

    def remote(src, dst, k, r):
        return pltpu.make_async_remote_copy(
            src_ref=src,
            dst_ref=dst,
            send_sem=send_sems.at[k],
            recv_sem=recv_sems.at[k],
            device_id=partner(r),
            device_id_type=pl.DeviceIdType.MESH,
        )

    def send(k, carry):
        r = lax.rem(me + lax.rem(k * SPREAD, ranks), ranks)
        remote(share, shares.at[me], 2, r).start()
        remote(out_cells.at[r], got_cells.at[me], 0, r).start()
        remote(out_body.at[r], got_body.at[me], 1, r).start()
        return carry

    lax.fori_loop(1, ranks, send, 0)

    whole = pl.ds(0, ranks - 1)
    later = lax.rem(me + 1, ranks)
    remote(shares.at[whole], shares.at[whole], 2, later).wait_recv()

    top = me // 2

    def weigh(t, total):
        pair = shares[2 * t] + shares[2 * t + 1]
        return total + weight_ref[top * tops + t] * pair

    coarse = lax.fori_loop(0, tops, weigh, jnp.zeros((2, LANES), F32))
    coarse = jnp.concatenate([coarse[0:1, :], coarse[1:2, :]], 1)
    coarse = jnp.broadcast_to(coarse, (16, width)).astype(BF16)
    for o in range(8):
        out = jnp.dot(coarse, down_ref[o], preferred_element_type=F32)
        far_ref[o : o + 1, :] = out[0:1, :]

    for copy in keep:
        copy.wait()
    remote(shares.at[whole], shares.at[whole], 2, later).wait_send()
    remote(out_cells.at[whole], got_cells.at[whole], 0, later).wait()
    remote(out_body.at[whole], got_body.at[whole], 1, later).wait()


def exchange(weight, share, downward_ops, out_cells, out_body):
    ranks, _, width = out_cells.shape
    smem = pl.BlockSpec(memory_space=pltpu.SMEM)
    vmem = pl.BlockSpec(memory_space=pltpu.VMEM)
    hbm = pl.BlockSpec(memory_space=pl.ANY)
    return pl.pallas_call(
        exchange_kernel,
        out_shape=(
            jax.ShapeDtypeStruct(out_cells.shape, BF16),
            jax.ShapeDtypeStruct(out_body.shape, F32),
            jax.ShapeDtypeStruct((8, width), F32),
        ),
        in_specs=[smem, vmem, vmem, hbm, hbm],
        out_specs=(hbm, hbm, vmem),
        scratch_shapes=[
            pltpu.VMEM((ranks, 2, LANES), F32),
            pltpu.SemaphoreType.DMA((3,)),
            pltpu.SemaphoreType.DMA((3,)),
            pltpu.SemaphoreType.DMA((2,)),
        ],
        compiler_params=pltpu.CompilerParams(
            collective_id=0,
            has_side_effects=True,
            vmem_limit_bytes=32 * 1024 * 1024,
        ),
    )(weight, share, downward_ops, out_cells, out_body)


def main_kernel(
    src_hbm,
    near_hbm,
    op_ref,
    own_ref,
    got_ref,
    ownp_ref,
    gotp_ref,
    far_ref,
    moves_ref,
    tr_hbm,
    local_ref,
    pot_ref,
    lower_ref,
    upper_ref,
    tab,
    charge,
    target,
    source,
    group_lo,
    group_hi,
    tr_ref,
    src_ref,
    near_ref,
    sems,
    *picked,
    list_width,
    op_count,
    pitch,
):
    cells = own_ref.shape[0]
    near_count = near_hbm.shape[0] // cells
    list_pad = op_ref.shape[1]
    src_copy = pltpu.make_async_copy(src_hbm, src_ref, sems.at[0])
    near_copy = pltpu.make_async_copy(near_hbm, near_ref, sems.at[1])
    tr_copy = pltpu.make_async_copy(tr_hbm, tr_ref, sems.at[2])
    near_copy.start()
    src_copy.start()
    tr_copy.start()
    for buf in picked:
        buf[...] = jnp.zeros_like(buf)

    halves_in_rows(own_ref, tab, 0)
    halves_in_rows(got_ref, tab, 2 * cells)

    group_lo[...] = jnp.zeros_like(group_lo)
    group_hi[...] = jnp.zeros_like(group_hi)

    def features(ref, first, stage, is_target):
        def step(i, carry):
            at = pl.multiple_of(i * 8, 8)
            block = [ref[pl.ds(at * 4 + a, 8, stride=4), :] for a in range(4)]
            axes = [pieces(b - 0.5, 2) for b in block[:3]]
            norm = jnp.zeros((8, LANES), F32)
            for high, low in axes:
                norm = norm + (high + low) * (high + low)
            one = jnp.ones((8, LANES), F32)
            highs = [a[0] for a in axes]
            lows = [a[1] for a in axes]
            if is_target:
                twice = [-2.0 * h for h in highs], [-2.0 * v for v in lows]
                rows = twice[0] * 2 + twice[1] * 2 + pieces(norm, 3) + [one] * 3
            else:
                rows = (highs + lows) * 2 + [one] * 3 + pieces(norm + SOFTENING, 3)
                charge[pl.ds(first + at, 8), :] = block[3]
            for k, row in enumerate(rows):
                stage[pl.ds(at * FEAT + k, 8, stride=FEAT), :] = row
            return carry

        lax.fori_loop(0, ref.shape[0] // 32, step, 0, unroll=4)

    def packed(stage, out, first, count):
        def step(i, carry):
            out[first + i] = stage[pl.ds(pl.multiple_of(i * FEAT, FEAT), FEAT), :].astype(BF16)
            return carry

        lax.fori_loop(0, count, step, 0, unroll=8)

    features(ownp_ref, 0, group_lo, True)
    packed(group_lo, target, 0, cells)
    features(ownp_ref, 0, group_hi, False)
    packed(group_hi, source, 0, cells)
    features(gotp_ref, cells, group_lo, False)
    packed(group_lo, source, cells, gotp_ref.shape[0] // 4)

    near_copy.wait()
    src_copy.wait()
    op_ids = lax.broadcasted_iota(jnp.int32, (op_count, list_pad), 0)

    def group(cell, buf):
        low = buf[pl.ds(0, list_pad, stride=2), :].astype(BF16)
        high = buf[pl.ds(1, list_pad, stride=2), :].astype(BF16)
        hot = jnp.where(op_ids == op_ref[pl.ds(cell, 1), :], 1.0, 0.0).astype(BF16)
        out = jnp.dot(hot, jnp.concatenate([low, high], 1), preferred_element_type=F32)
        group_lo[pl.ds(cell, op_count, stride=pitch), :] = out[:, :LANES]
        group_hi[pl.ds(cell, op_count, stride=pitch), :] = out[:, LANES:]

    def reduced(total, cell):
        pot_ref[pl.ds(cell, 1), :] = jnp.sum(total.T, axis=0, keepdims=True)

    per_pair = -(-list_width // ((near_count + 1) // 2))

    def leaves(c, carry):
        pending = None
        for u in range(UNROLL):
            cell = c * UNROLL + u
            x = target[cell]
            src_at = cell * list_width
            near_at = cell * near_count
            total = jnp.zeros((LANES, LANES), F32)
            taken = 0
            for p in range(0, near_count, 2):
                for j in range(taken, min(taken + per_pair, list_width)):
                    row = pl.multiple_of(src_ref[src_at + j], 2)
                    picked[u][2 * j : 2 * j + 2, :] = tab[pl.ds(row, 2), :]
                taken += per_pair
                ids = [near_ref[near_at + n] for n in range(p, min(p + 2, near_count))]
                y = [source[i] for i in ids]
                y = jnp.concatenate(y, axis=1) if len(y) > 1 else y[0]
                dist = lax.dot_general(
                    x, y, (((0,), (0,)), ((), ())), preferred_element_type=F32
                )
                for t, i in enumerate(ids):
                    part = lax.rsqrt(dist[:, t * LANES : (t + 1) * LANES])
                    total = total + part * charge[pl.ds(i, 1), :]
                if p == 4:
                    group(jnp.maximum(cell - 1, 0), picked[(u - 1) % UNROLL])
                if p == 8 and pending is not None:
                    reduced(*pending)
            pending = (total, cell)
        reduced(*pending)
        return carry

    lax.fori_loop(0, cells // UNROLL, leaves, 0)
    group(cells - 1, picked[UNROLL - 1])

    for out, column in ((lower_ref, 0), (upper_ref, 1)):
        for s in range(MCAP):
            leaf = s if column == 0 else cells - 1 - s
            kept = s < moves_ref[0, column]
            block = ownp_ref[4 * leaf : 4 * leaf + 4, :]
            out[s, 0:4, :] = jnp.where(kept, block, 0.0)
            out[s, 4:5, :] = jnp.where(kept, pot_ref[leaf : leaf + 1, :], 0.0)

    tr_copy.wait()
    far = jnp.concatenate([far_ref[...]] * (cells // 8), 0)
    local_ref[...] = far
    width = 2 * LANES

    def translate(k, carry):
        parts = []
        for kk in range(KSTEP):
            at = pl.ds(pl.multiple_of((k * KSTEP + kk) * pitch, 8), cells)
            parts += [group_lo[at, :].astype(BF16), group_hi[at, :].astype(BF16)]
        ops = tr_ref[pl.ds(k * KSTEP, KSTEP)].reshape(KSTEP * width, width)
        local_ref[...] += jnp.dot(
            jnp.concatenate(parts, 1), ops, preferred_element_type=F32
        )
        return carry

    lax.fori_loop(0, op_count // KSTEP, translate, 0)


def main_call(src, near, ops, own, got, own_p, got_p, far, moves, translate_ops):
    cells = own.shape[0]
    list_width = src.shape[0] // cells
    list_pad = ops.shape[1]
    op_count = translate_ops.shape[0]
    tables = cells + got_p.shape[0] // 4
    pitch = cells + 8
    hbm = pl.BlockSpec(memory_space=pl.ANY)
    vmem = pl.BlockSpec(memory_space=pltpu.VMEM)
    return pl.pallas_call(
        functools.partial(
            main_kernel, list_width=list_width, op_count=op_count, pitch=pitch
        ),
        out_shape=(
            jax.ShapeDtypeStruct((cells, 2 * LANES), F32),
            jax.ShapeDtypeStruct((cells, LANES), F32),
            jax.ShapeDtypeStruct((MCAP, 5, LANES), F32),
            jax.ShapeDtypeStruct((MCAP, 5, LANES), F32),
        ),
        in_specs=[hbm, hbm] + [vmem] * 6 + [pl.BlockSpec(memory_space=pltpu.SMEM), hbm],
        out_specs=(vmem,) * 4,
        scratch_shapes=[
            pltpu.VMEM((2 * (cells + got.shape[0]), LANES), F32),
            pltpu.VMEM((tables, LANES), F32),
            pltpu.VMEM((cells, FEAT, LANES), BF16),
            pltpu.VMEM((tables, FEAT, LANES), BF16),
            pltpu.VMEM((op_count * pitch, LANES), F32),
            pltpu.VMEM((op_count * pitch, LANES), F32),
            pltpu.VMEM(translate_ops.shape, BF16),
            pltpu.SMEM(src.shape, jnp.int32),
            pltpu.SMEM(near.shape, jnp.int32),
            pltpu.SemaphoreType.DMA((3,)),
        ]
        + [pltpu.VMEM((2 * list_pad, LANES), F32)] * UNROLL,
        compiler_params=pltpu.CompilerParams(vmem_limit_bytes=60 * 1024 * 1024),
    )(src, near, ops, own, got, own_p, got_p, far, moves, translate_ops)


def per_device(
    multipole,
    positions,
    charges,
    translate_ops,
    upward_ops,
    downward_ops,
    top_weight,
    send_cells,
    send_leaves,
    list_source,
    list_operator,
    near_leaves,
    move_counts,
):
    cells, width = multipole.shape
    leaf_size = positions.shape[2]
    ranks = lax.axis_size(AXES)

    body = jnp.concatenate([positions, charges[:, None, :]], 1)
    flat = body.reshape(-1, leaf_size)
    out_cells, out_body, share = pack(
        (send_cells * 2).reshape(-1),
        (send_leaves * 4).reshape(-1),
        multipole,
        flat,
        upward_ops,
        ranks,
    )
    got_cells, got_body, far = exchange(
        top_weight.reshape(-1), share, downward_ops, out_cells, out_body
    )
    list_pad = -(-list_operator.shape[1] // 64) * 64
    ops = jnp.pad(
        list_operator,
        ((0, 0), (0, list_pad - list_operator.shape[1])),
        constant_values=translate_ops.shape[0],
    )
    local_exp, potential, lower, upper = main_call(
        (list_source * 2).reshape(-1),
        near_leaves.reshape(-1),
        ops,
        multipole,
        got_cells.reshape(-1, width),
        flat,
        got_body.reshape(-1, leaf_size),
        far,
        move_counts,
        translate_ops,
    )

    from_upper = shifted(lower, AXES, -1)
    from_lower = shifted(upper, AXES, 1)
    arrivals = jnp.concatenate([from_upper, from_lower], 0)
    return (local_exp, potential, arrivals)


def solution(mesh):
    rows = P(AXES, None)
    blocks = P(AXES, None, None)
    placed = (rows, blocks, rows) + (P(),) * 4 + (rows,) * 6
    return jax.shard_map(
        per_device,
        mesh=mesh,
        in_specs=placed,
        out_specs=(rows, rows, blocks),
        check_vma=False,
    )
```

```python
import functools

import jax
import jax.numpy as jnp
from jax import lax
from jax.experimental import pallas as pl
from jax.experimental.pallas import tpu as pltpu
from jax.sharding import PartitionSpec as P

F32 = jnp.float32
BF16 = jnp.bfloat16
MCAP = 8
SOFTENING = 0.01
AXES = ("leaf", "sub")
LANES = 128
FEAT = 32
UNROLL = 16
KSTEP = 8
WINDOW = 8
SPREAD = 45


def shifted(x, axis, by):
    devices = lax.axis_size(axis)
    pairs = [(i, i + by) for i in range(devices) if 0 <= i + by < devices]
    return lax.ppermute(x, axis, pairs)


def pieces(x, count):
    out = []
    for _ in range(count):
        head = x.astype(BF16).astype(F32)
        out.append(head)
        x = x - head
    return out


def partner(rank):
    subs = lax.axis_size("sub")
    return (rank // subs, lax.rem(rank, subs))


def halves_in_rows(ref, out, base):
    def step(i, carry):
        rows = ref[pl.ds(pl.multiple_of(i * 16, 16), 16), :].astype(F32)
        at = base + i * 32
        out[pl.ds(at, 16, stride=2), :] = rows[:, :LANES]
        out[pl.ds(at + 1, 16, stride=2), :] = rows[:, LANES:]
        return carry

    lax.fori_loop(0, ref.shape[0] // 16, step, 0, unroll=4)


def pack_kernel(
    cell_ids, leaf_ids, own_ref, body_ref, up_ref, out_cells, out_body, share, tab, stage
):
    ranks, cap, width = out_cells.shape
    blocks = out_body.shape[1] // 4
    halves_in_rows(own_ref, tab, 0)

    def pick(r, carry):
        for s in range(cap):
            row = pl.multiple_of(cell_ids[r * cap + s], 2)
            stage[pl.ds(r * 2 * cap + 2 * s, 2), :] = tab[pl.ds(row, 2), :]
        for s in range(blocks):
            row = pl.multiple_of(leaf_ids[r * blocks + s], 4)
            out_body[r, 4 * s : 4 * s + 4, :] = body_ref[pl.ds(row, 4), :]
        return carry

    lax.fori_loop(0, ranks, pick, 0, unroll=2)

    def pack(r, carry):
        low = stage[pl.ds(r * 2 * cap, cap, stride=2), :]
        high = stage[pl.ds(r * 2 * cap + 1, cap, stride=2), :]
        out_cells[r] = jnp.concatenate([low, high], 1).astype(BF16)
        return carry

    lax.fori_loop(0, ranks, pack, 0, unroll=4)

    rows = own_ref.shape[0]
    octants = jnp.sum(own_ref[...].astype(F32).reshape(rows // 8, 8, width), axis=0)
    lhs = jnp.concatenate(pieces(octants, 3) + [jnp.zeros((8, width), F32)], 0)
    lhs = lhs.astype(BF16)
    row_octant = lax.rem(lax.broadcasted_iota(jnp.int32, (32, width), 0), 8)

    def lift(o, total):
        out = jnp.dot(lhs, up_ref[o], preferred_element_type=F32)
        return total + jnp.where(row_octant == o, out, 0.0)

    lifted = lax.fori_loop(0, 8, lift, jnp.zeros((32, width), F32), unroll=True)
    lifted = jnp.sum(lifted, axis=0, keepdims=True)
    share[0:1, :] = lifted[:, :LANES]
    share[1:2, :] = lifted[:, LANES:]


def pack(cell_ids, leaf_ids, own, body, upward_ops, ranks):
    width = own.shape[1]
    cap = cell_ids.shape[0] // ranks
    rows = 4 * (leaf_ids.shape[0] // ranks)
    smem = pl.BlockSpec(memory_space=pltpu.SMEM)
    vmem = pl.BlockSpec(memory_space=pltpu.VMEM)
    return pl.pallas_call(
        pack_kernel,
        out_shape=(
            jax.ShapeDtypeStruct((ranks, cap, width), BF16),
            jax.ShapeDtypeStruct((ranks, rows, LANES), F32),
            jax.ShapeDtypeStruct((2, LANES), F32),
        ),
        in_specs=[smem] * 2 + [vmem] * 3,
        out_specs=(vmem,) * 3,
        scratch_shapes=[
            pltpu.VMEM((2 * own.shape[0], LANES), F32),
            pltpu.VMEM((ranks * 2 * cap, LANES), F32),
        ],
        compiler_params=pltpu.CompilerParams(vmem_limit_bytes=32 * 1024 * 1024),
    )(cell_ids, leaf_ids, own, body, upward_ops)


def exchange_kernel(
    weight_ref,
    share,
    down_ref,
    out_cells,
    out_body,
    got_cells,
    got_body,
    far_ref,
    shares,
    send_sems,
    recv_sems,
    local_sems,
):
    me = lax.axis_index(AXES)
    ranks = shares.shape[0]
    tops = ranks // 2
    width = 2 * LANES
    barrier = pltpu.get_barrier_semaphore()

    def greet(d, carry):
        pl.semaphore_signal(
            barrier,
            inc=1,
            device_id=partner(lax.rem(me + d, ranks)),
            device_id_type=pl.DeviceIdType.MESH,
        )
        return carry

    lax.fori_loop(1, ranks, greet, 0)
    keep = [
        pltpu.make_async_copy(out_cells.at[me], got_cells.at[me], local_sems.at[0]),
        pltpu.make_async_copy(out_body.at[me], got_body.at[me], local_sems.at[1]),
    ]
    for copy in keep:
        copy.start()
    shares[me] = share[...]
    pl.semaphore_wait(barrier, ranks - 1)

    def remote(src, dst, k, r):
        return pltpu.make_async_remote_copy(
            src_ref=src,
            dst_ref=dst,
            send_sem=send_sems.at[k],
            recv_sem=recv_sems.at[k],
            device_id=partner(r),
            device_id_type=pl.DeviceIdType.MESH,
        )

    def send(k, carry):
        r = lax.rem(me + lax.rem(k * SPREAD, ranks), ranks)
        remote(share, shares.at[me], 2, r).start()
        remote(out_cells.at[r], got_cells.at[me], 0, r).start()
        remote(out_body.at[r], got_body.at[me], 1, r).start()
        return carry

    lax.fori_loop(1, ranks, send, 0)

    whole = pl.ds(0, ranks - 1)
    later = lax.rem(me + 1, ranks)
    remote(shares.at[whole], shares.at[whole], 2, later).wait_recv()

    top = me // 2

    def weigh(t, total):
        pair = shares[2 * t] + shares[2 * t + 1]
        return total + weight_ref[top * tops + t] * pair

    coarse = lax.fori_loop(0, tops, weigh, jnp.zeros((2, LANES), F32))
    coarse = jnp.concatenate([coarse[0:1, :], coarse[1:2, :]], 1)
    coarse = jnp.broadcast_to(coarse, (16, width)).astype(BF16)
    for o in range(8):
        out = jnp.dot(coarse, down_ref[o], preferred_element_type=F32)
        far_ref[o : o + 1, :] = out[0:1, :]

    for copy in keep:
        copy.wait()
    remote(shares.at[whole], shares.at[whole], 2, later).wait_send()
    remote(out_cells.at[whole], got_cells.at[whole], 0, later).wait()
    remote(out_body.at[whole], got_body.at[whole], 1, later).wait()


def exchange(weight, share, downward_ops, out_cells, out_body):
    ranks, _, width = out_cells.shape
    smem = pl.BlockSpec(memory_space=pltpu.SMEM)
    vmem = pl.BlockSpec(memory_space=pltpu.VMEM)
    hbm = pl.BlockSpec(memory_space=pl.ANY)
    return pl.pallas_call(
        exchange_kernel,
        out_shape=(
            jax.ShapeDtypeStruct(out_cells.shape, BF16),
            jax.ShapeDtypeStruct(out_body.shape, F32),
            jax.ShapeDtypeStruct((8, width), F32),
        ),
        in_specs=[smem, vmem, vmem, hbm, hbm],
        out_specs=(hbm, hbm, vmem),
        scratch_shapes=[
            pltpu.VMEM((ranks, 2, LANES), F32),
            pltpu.SemaphoreType.DMA((3,)),
            pltpu.SemaphoreType.DMA((3,)),
            pltpu.SemaphoreType.DMA((2,)),
        ],
        compiler_params=pltpu.CompilerParams(
            collective_id=0,
            has_side_effects=True,
            vmem_limit_bytes=32 * 1024 * 1024,
        ),
    )(weight, share, downward_ops, out_cells, out_body)


def main_kernel(
    src_hbm,
    near_hbm,
    op_ref,
    own_ref,
    got_ref,
    ownp_ref,
    gotp_ref,
    far_ref,
    moves_ref,
    tr_hbm,
    local_ref,
    pot_ref,
    lower_ref,
    upper_ref,
    tab,
    charge,
    target,
    source,
    group_lo,
    group_hi,
    tr_ref,
    window_a,
    window_b,
    near_ref,
    sems,
    *picked,
    list_width,
    op_count,
    pitch,
):
    cells = own_ref.shape[0]
    near_count = near_hbm.shape[0] // cells
    list_pad = op_ref.shape[1]
    windows = (window_a, window_b)
    span = window_a.shape[0]

    def fetch(slot, block):
        at = pl.multiple_of(block * span, span)
        return pltpu.make_async_copy(
            src_hbm.at[pl.ds(at, span)], windows[slot], sems.at[3 * slot]
        )

    near_copy = pltpu.make_async_copy(near_hbm, near_ref, sems.at[1])
    tr_copy = pltpu.make_async_copy(tr_hbm, tr_ref, sems.at[2])
    near_copy.start()
    fetch(0, 0).start()
    fetch(1, 1).start()
    tr_copy.start()
    for buf in picked:
        buf[...] = jnp.zeros_like(buf)

    halves_in_rows(own_ref, tab, 0)
    halves_in_rows(got_ref, tab, 2 * cells)

    group_lo[...] = jnp.zeros_like(group_lo)
    group_hi[...] = jnp.zeros_like(group_hi)

    def features(ref, first, stage, is_target):
        def step(i, carry):
            at = pl.multiple_of(i * 8, 8)
            block = [ref[pl.ds(at * 4 + a, 8, stride=4), :] for a in range(4)]
            axes = [pieces(b - 0.5, 2) for b in block[:3]]
            norm = jnp.zeros((8, LANES), F32)
            for high, low in axes:
                norm = norm + (high + low) * (high + low)
            one = jnp.ones((8, LANES), F32)
            highs = [a[0] for a in axes]
            lows = [a[1] for a in axes]
            if is_target:
                twice = [-2.0 * h for h in highs], [-2.0 * v for v in lows]
                rows = twice[0] * 2 + twice[1] * 2 + pieces(norm, 3) + [one] * 3
            else:
                rows = (highs + lows) * 2 + [one] * 3 + pieces(norm + SOFTENING, 3)
                charge[pl.ds(first + at, 8), :] = block[3]
            for k, row in enumerate(rows):
                stage[pl.ds(at * FEAT + k, 8, stride=FEAT), :] = row
            return carry

        lax.fori_loop(0, ref.shape[0] // 32, step, 0, unroll=4)

    def packed(stage, out, first, count):
        def step(i, carry):
            out[first + i] = stage[pl.ds(pl.multiple_of(i * FEAT, FEAT), FEAT), :].astype(BF16)
            return carry

        lax.fori_loop(0, count, step, 0, unroll=8)

    features(ownp_ref, 0, group_lo, True)
    packed(group_lo, target, 0, cells)
    features(ownp_ref, 0, group_hi, False)
    packed(group_hi, source, 0, cells)
    features(gotp_ref, cells, group_lo, False)
    packed(group_lo, source, cells, gotp_ref.shape[0] // 4)

    near_copy.wait()
    op_ids = lax.broadcasted_iota(jnp.int32, (op_count, list_pad), 0)

    def group(cell, buf):
        low = buf[pl.ds(0, list_pad, stride=2), :].astype(BF16)
        high = buf[pl.ds(1, list_pad, stride=2), :].astype(BF16)
        hot = jnp.where(op_ids == op_ref[pl.ds(cell, 1), :], 1.0, 0.0).astype(BF16)
        out = jnp.dot(hot, jnp.concatenate([low, high], 1), preferred_element_type=F32)
        group_lo[pl.ds(cell, op_count, stride=pitch), :] = out[:, :LANES]
        group_hi[pl.ds(cell, op_count, stride=pitch), :] = out[:, LANES:]

    def reduced(total, cell):
        pot_ref[pl.ds(cell, 1), :] = jnp.sum(total.T, axis=0, keepdims=True)

    per_pair = -(-list_width // ((near_count + 1) // 2))

    def leaves(c, carry):
        pending = None
        for u in range(UNROLL):
            cell = c * UNROLL + u
            x = target[cell]
            slot = u // WINDOW
            if u % WINDOW == 0:
                fetch(slot, 2 * c + slot).wait()
            src_at = (u % WINDOW) * list_width
            near_at = cell * near_count
            total = jnp.zeros((LANES, LANES), F32)
            taken = 0
            for p in range(0, near_count, 2):
                for j in range(taken, min(taken + per_pair, list_width)):
                    row = pl.multiple_of(windows[slot][src_at + j], 2)
                    picked[u][2 * j : 2 * j + 2, :] = tab[pl.ds(row, 2), :]
                taken += per_pair
                ids = [near_ref[near_at + n] for n in range(p, min(p + 2, near_count))]
                y = [source[i] for i in ids]
                y = jnp.concatenate(y, axis=1) if len(y) > 1 else y[0]
                dist = lax.dot_general(
                    x, y, (((0,), (0,)), ((), ())), preferred_element_type=F32
                )
                for t, i in enumerate(ids):
                    part = lax.rsqrt(dist[:, t * LANES : (t + 1) * LANES])
                    total = total + part * charge[pl.ds(i, 1), :]
                if p == 4:
                    group(jnp.maximum(cell - 1, 0), picked[(u - 1) % UNROLL])
                if p == 8 and pending is not None:
                    reduced(*pending)
            pending = (total, cell)
            if u % WINDOW == WINDOW - 1:

                @pl.when(c + 1 < cells // UNROLL)
                def _():
                    fetch(slot, 2 * (c + 1) + slot).start()

        reduced(*pending)
        return carry

    lax.fori_loop(0, cells // UNROLL, leaves, 0)
    group(cells - 1, picked[UNROLL - 1])

    for out, column in ((lower_ref, 0), (upper_ref, 1)):
        for s in range(MCAP):
            leaf = s if column == 0 else cells - 1 - s
            kept = s < moves_ref[0, column]
            block = ownp_ref[4 * leaf : 4 * leaf + 4, :]
            out[s, 0:4, :] = jnp.where(kept, block, 0.0)
            out[s, 4:5, :] = jnp.where(kept, pot_ref[leaf : leaf + 1, :], 0.0)

    tr_copy.wait()
    far = jnp.concatenate([far_ref[...]] * (cells // 8), 0)
    local_ref[...] = far
    width = 2 * LANES

    def translate(k, carry):
        parts = []
        for kk in range(KSTEP):
            at = pl.ds(pl.multiple_of((k * KSTEP + kk) * pitch, 8), cells)
            parts += [group_lo[at, :].astype(BF16), group_hi[at, :].astype(BF16)]
        ops = tr_ref[pl.ds(k * KSTEP, KSTEP)].reshape(KSTEP * width, width)
        local_ref[...] += jnp.dot(
            jnp.concatenate(parts, 1), ops, preferred_element_type=F32
        )
        return carry

    lax.fori_loop(0, op_count // KSTEP, translate, 0)


def main_call(list_width, src, near, ops, own, got, own_p, got_p, far, moves, translate_ops):
    cells = own.shape[0]
    list_pad = ops.shape[1]
    op_count = translate_ops.shape[0]
    tables = cells + got_p.shape[0] // 4
    pitch = cells + 8
    hbm = pl.BlockSpec(memory_space=pl.ANY)
    vmem = pl.BlockSpec(memory_space=pltpu.VMEM)
    return pl.pallas_call(
        functools.partial(
            main_kernel, list_width=list_width, op_count=op_count, pitch=pitch
        ),
        out_shape=(
            jax.ShapeDtypeStruct((cells, 2 * LANES), F32),
            jax.ShapeDtypeStruct((cells, LANES), F32),
            jax.ShapeDtypeStruct((MCAP, 5, LANES), F32),
            jax.ShapeDtypeStruct((MCAP, 5, LANES), F32),
        ),
        in_specs=[hbm, hbm] + [vmem] * 6 + [pl.BlockSpec(memory_space=pltpu.SMEM), hbm],
        out_specs=(vmem,) * 4,
        scratch_shapes=[
            pltpu.VMEM((2 * (cells + got.shape[0]), LANES), F32),
            pltpu.VMEM((tables, LANES), F32),
            pltpu.VMEM((cells, FEAT, LANES), BF16),
            pltpu.VMEM((tables, FEAT, LANES), BF16),
            pltpu.VMEM((op_count * pitch, LANES), F32),
            pltpu.VMEM((op_count * pitch, LANES), F32),
            pltpu.VMEM(translate_ops.shape, BF16),
            pltpu.SMEM((src.shape[0] * WINDOW // cells,), jnp.int32),
            pltpu.SMEM((src.shape[0] * WINDOW // cells,), jnp.int32),
            pltpu.SMEM(near.shape, jnp.int32),
            pltpu.SemaphoreType.DMA((4,)),
        ]
        + [pltpu.VMEM((2 * list_pad, LANES), F32)] * UNROLL,
        compiler_params=pltpu.CompilerParams(vmem_limit_bytes=60 * 1024 * 1024),
    )(src, near, ops, own, got, own_p, got_p, far, moves, translate_ops)


def per_device(
    multipole,
    positions,
    charges,
    translate_ops,
    upward_ops,
    downward_ops,
    top_weight,
    send_cells,
    send_leaves,
    list_source,
    list_operator,
    near_leaves,
    move_counts,
):
    cells, width = multipole.shape
    leaf_size = positions.shape[2]
    ranks = lax.axis_size(AXES)

    body = jnp.concatenate([positions, charges[:, None, :]], 1)
    flat = body.reshape(-1, leaf_size)
    out_cells, out_body, share = pack(
        (send_cells * 2).reshape(-1),
        (send_leaves * 4).reshape(-1),
        multipole,
        flat,
        upward_ops,
        ranks,
    )
    got_cells, got_body, far = exchange(
        top_weight.reshape(-1), share, downward_ops, out_cells, out_body
    )
    list_pad = -(-list_operator.shape[1] // 64) * 64
    ops = jnp.pad(
        list_operator,
        ((0, 0), (0, list_pad - list_operator.shape[1])),
        constant_values=translate_ops.shape[0],
    )
    flat_lists = (list_source * 2).reshape(cells // WINDOW, -1)
    span = -(-flat_lists.shape[1] // 1024) * 1024
    flat_lists = jnp.pad(flat_lists, ((0, 0), (0, span - flat_lists.shape[1])))
    local_exp, potential, lower, upper = main_call(
        list_source.shape[1],
        flat_lists.reshape(-1),
        near_leaves.reshape(-1),
        ops,
        multipole,
        got_cells.reshape(-1, width),
        flat,
        got_body.reshape(-1, leaf_size),
        far,
        move_counts,
        translate_ops,
    )

    from_upper = shifted(lower, AXES, -1)
    from_lower = shifted(upper, AXES, 1)
    arrivals = jnp.concatenate([from_upper, from_lower], 0)
    return (local_exp, potential, arrivals)


def solution(mesh):
    rows = P(AXES, None)
    blocks = P(AXES, None, None)
    placed = (rows, blocks, rows) + (P(),) * 4 + (rows,) * 6
    return jax.shard_map(
        per_device,
        mesh=mesh,
        in_specs=placed,
        out_specs=(rows, rows, blocks),
        check_vma=False,
    )
```

```python
import functools

import jax
import jax.numpy as jnp
from jax import lax
from jax.experimental import pallas as pl
from jax.experimental.pallas import tpu as pltpu
from jax.sharding import PartitionSpec as P

F32 = jnp.float32
BF16 = jnp.bfloat16
MCAP = 8
SOFTENING = 0.01
AXES = ("leaf", "sub")
LANES = 128
FEAT = 32
UNROLL = 16
KSTEP = 8
WINDOW = 8
PLACE_STEPS = 65535.0
CHARGE_STEPS = 32767.0
SPREAD = 45


def shifted(x, axis, by):
    devices = lax.axis_size(axis)
    pairs = [(i, i + by) for i in range(devices) if 0 <= i + by < devices]
    return lax.ppermute(x, axis, pairs)


def pieces(x, count):
    out = []
    for _ in range(count):
        head = x.astype(BF16).astype(F32)
        out.append(head)
        x = x - head
    return out


def partner(rank):
    subs = lax.axis_size("sub")
    return (rank // subs, lax.rem(rank, subs))


def halves_in_rows(ref, out, base):
    def step(i, carry):
        rows = ref[pl.ds(pl.multiple_of(i * 16, 16), 16), :].astype(F32)
        at = base + i * 32
        out[pl.ds(at, 16, stride=2), :] = rows[:, :LANES]
        out[pl.ds(at + 1, 16, stride=2), :] = rows[:, LANES:]
        return carry

    lax.fori_loop(0, ref.shape[0] // 16, step, 0, unroll=4)


def charge_rows(rows):
    return lax.rem(lax.broadcasted_iota(jnp.int32, (rows, LANES), 0), 4) == 3


def pack_kernel(
    cell_ids,
    leaf_ids,
    own_ref,
    body_ref,
    up_ref,
    out_cells,
    out_body,
    share,
    tab,
    stage,
    stage_body,
):
    ranks, cap, width = out_cells.shape
    blocks = out_body.shape[1] // 4
    halves_in_rows(own_ref, tab, 0)

    def pick(r, carry):
        for s in range(cap):
            row = pl.multiple_of(cell_ids[r * cap + s], 2)
            stage[pl.ds(r * 2 * cap + 2 * s, 2), :] = tab[pl.ds(row, 2), :]
        for s in range(blocks):
            row = pl.multiple_of(leaf_ids[r * blocks + s], 4)
            at = r * 4 * blocks + 4 * s
            stage_body[pl.ds(at, 4), :] = body_ref[pl.ds(row, 4), :]
        return carry

    lax.fori_loop(0, ranks, pick, 0, unroll=2)

    leaves = body_ref.shape[0] // 4
    biggest = jnp.max(jnp.abs(body_ref[pl.ds(3, leaves, stride=4), :]), axis=0, keepdims=True)
    biggest = jnp.max(biggest, axis=1, keepdims=True)
    biggest = jnp.maximum(jnp.broadcast_to(biggest, (1, LANES)), 1e-30)
    per_unit = CHARGE_STEPS / biggest
    rows_out = 4 * blocks
    is_charge = charge_rows(rows_out)

    def pack(r, carry):
        raw = stage_body[pl.ds(pl.multiple_of(r * rows_out, rows_out), rows_out), :]
        code = jnp.where(is_charge, raw * per_unit + 32768.5, raw * PLACE_STEPS + 0.5)
        out_body[r] = (code.astype(jnp.int32) - 32768).astype(jnp.int16)
        low = stage[pl.ds(r * 2 * cap, cap, stride=2), :]
        high = stage[pl.ds(r * 2 * cap + 1, cap, stride=2), :]
        out_cells[r] = jnp.concatenate([low, high], 1).astype(BF16)
        return carry

    lax.fori_loop(0, ranks, pack, 0, unroll=4)

    rows = own_ref.shape[0]
    octants = jnp.sum(own_ref[...].astype(F32).reshape(rows // 8, 8, width), axis=0)
    lhs = jnp.concatenate(pieces(octants, 3) + [jnp.zeros((8, width), F32)], 0)
    lhs = lhs.astype(BF16)
    row_octant = lax.rem(lax.broadcasted_iota(jnp.int32, (32, width), 0), 8)

    def lift(o, total):
        out = jnp.dot(lhs, up_ref[o], preferred_element_type=F32)
        return total + jnp.where(row_octant == o, out, 0.0)

    lifted = lax.fori_loop(0, 8, lift, jnp.zeros((32, width), F32), unroll=True)
    lifted = jnp.sum(lifted, axis=0, keepdims=True)
    share[0:1, :] = lifted[:, :LANES]
    share[1:2, :] = lifted[:, LANES:]
    share[2:3, :] = biggest
    share[3:4, :] = jnp.zeros((1, LANES), F32)


def pack(cell_ids, leaf_ids, own, body, upward_ops, ranks):
    width = own.shape[1]
    cap = cell_ids.shape[0] // ranks
    rows = 4 * (leaf_ids.shape[0] // ranks)
    smem = pl.BlockSpec(memory_space=pltpu.SMEM)
    vmem = pl.BlockSpec(memory_space=pltpu.VMEM)
    return pl.pallas_call(
        pack_kernel,
        out_shape=(
            jax.ShapeDtypeStruct((ranks, cap, width), BF16),
            jax.ShapeDtypeStruct((ranks, rows, LANES), jnp.int16),
            jax.ShapeDtypeStruct((4, LANES), F32),
        ),
        in_specs=[smem] * 2 + [vmem] * 3,
        out_specs=(vmem,) * 3,
        scratch_shapes=[
            pltpu.VMEM((2 * own.shape[0], LANES), F32),
            pltpu.VMEM((ranks * 2 * cap, LANES), F32),
            pltpu.VMEM((ranks * rows, LANES), F32),
        ],
        compiler_params=pltpu.CompilerParams(vmem_limit_bytes=32 * 1024 * 1024),
    )(cell_ids, leaf_ids, own, body, upward_ops)


def exchange_kernel(
    weight_ref,
    share,
    down_ref,
    out_cells,
    out_body,
    got_cells,
    got_body,
    far_ref,
    scale_ref,
    shares,
    send_sems,
    recv_sems,
    local_sems,
):
    me = lax.axis_index(AXES)
    ranks = shares.shape[0]
    tops = ranks // 2
    width = 2 * LANES
    barrier = pltpu.get_barrier_semaphore()

    def greet(d, carry):
        pl.semaphore_signal(
            barrier,
            inc=1,
            device_id=partner(lax.rem(me + d, ranks)),
            device_id_type=pl.DeviceIdType.MESH,
        )
        return carry

    lax.fori_loop(1, ranks, greet, 0)
    keep = [
        pltpu.make_async_copy(out_cells.at[me], got_cells.at[me], local_sems.at[0]),
        pltpu.make_async_copy(out_body.at[me], got_body.at[me], local_sems.at[1]),
    ]
    for copy in keep:
        copy.start()
    shares[me] = share[...]
    pl.semaphore_wait(barrier, ranks - 1)

    def remote(src, dst, k, r):
        return pltpu.make_async_remote_copy(
            src_ref=src,
            dst_ref=dst,
            send_sem=send_sems.at[k],
            recv_sem=recv_sems.at[k],
            device_id=partner(r),
            device_id_type=pl.DeviceIdType.MESH,
        )

    def send(k, carry):
        r = lax.rem(me + lax.rem(k * SPREAD, ranks), ranks)
        remote(share, shares.at[me], 2, r).start()
        remote(out_cells.at[r], got_cells.at[me], 0, r).start()
        remote(out_body.at[r], got_body.at[me], 1, r).start()
        return carry

    lax.fori_loop(1, ranks, send, 0)

    whole = pl.ds(0, ranks - 1)
    later = lax.rem(me + 1, ranks)
    remote(shares.at[whole], shares.at[whole], 2, later).wait_recv()

    top = me // 2

    def weigh(t, total):
        pair = shares[2 * t] + shares[2 * t + 1]
        return total + weight_ref[top * tops + t] * pair

    coarse = lax.fori_loop(0, tops, weigh, jnp.zeros((4, LANES), F32))
    coarse = jnp.concatenate([coarse[0:1, :], coarse[1:2, :]], 1)
    coarse = jnp.broadcast_to(coarse, (16, width)).astype(BF16)
    for o in range(8):
        out = jnp.dot(coarse, down_ref[o], preferred_element_type=F32)
        far_ref[o : o + 1, :] = out[0:1, :]


    def keep_scale(r, carry):
        scale_ref[pl.ds(r, 1), :] = shares[r, 2:3, :]
        return carry

    lax.fori_loop(0, ranks, keep_scale, 0)

    for copy in keep:
        copy.wait()
    remote(shares.at[whole], shares.at[whole], 2, later).wait_send()
    remote(out_cells.at[whole], got_cells.at[whole], 0, later).wait()
    remote(out_body.at[whole], got_body.at[whole], 1, later).wait()


def exchange(weight, share, downward_ops, out_cells, out_body):
    ranks, _, width = out_cells.shape
    smem = pl.BlockSpec(memory_space=pltpu.SMEM)
    vmem = pl.BlockSpec(memory_space=pltpu.VMEM)
    hbm = pl.BlockSpec(memory_space=pl.ANY)
    return pl.pallas_call(
        exchange_kernel,
        out_shape=(
            jax.ShapeDtypeStruct(out_cells.shape, BF16),
            jax.ShapeDtypeStruct(out_body.shape, jnp.int16),
            jax.ShapeDtypeStruct((8, width), F32),
            jax.ShapeDtypeStruct((ranks, LANES), F32),
        ),
        in_specs=[smem, vmem, vmem, hbm, hbm],
        out_specs=(hbm, hbm, vmem, vmem),
        scratch_shapes=[
            pltpu.VMEM((ranks, 4, LANES), F32),
            pltpu.SemaphoreType.DMA((3,)),
            pltpu.SemaphoreType.DMA((3,)),
            pltpu.SemaphoreType.DMA((2,)),
        ],
        compiler_params=pltpu.CompilerParams(
            collective_id=0,
            has_side_effects=True,
            vmem_limit_bytes=32 * 1024 * 1024,
        ),
    )(weight, share, downward_ops, out_cells, out_body)


def main_kernel(
    src_hbm,
    near_hbm,
    op_ref,
    own_ref,
    got_ref,
    ownp_ref,
    coded_ref,
    scale_ref,
    far_ref,
    moves_ref,
    tr_hbm,
    local_ref,
    pot_ref,
    lower_ref,
    upper_ref,
    tab,
    charge,
    target,
    source,
    group_lo,
    group_hi,
    tr_ref,
    window_a,
    window_b,
    near_ref,
    sems,
    gotp_ref,
    *picked,
    list_width,
    op_count,
    pitch,
):
    cells = own_ref.shape[0]
    near_count = near_hbm.shape[0] // cells
    list_pad = op_ref.shape[1]
    windows = (window_a, window_b)
    span = window_a.shape[0]

    def fetch(slot, block):
        at = pl.multiple_of(block * span, span)
        return pltpu.make_async_copy(
            src_hbm.at[pl.ds(at, span)], windows[slot], sems.at[3 * slot]
        )

    near_copy = pltpu.make_async_copy(near_hbm, near_ref, sems.at[1])
    tr_copy = pltpu.make_async_copy(tr_hbm, tr_ref, sems.at[2])
    near_copy.start()
    fetch(0, 0).start()
    fetch(1, 1).start()
    tr_copy.start()
    for buf in picked:
        buf[...] = jnp.zeros_like(buf)

    halves_in_rows(own_ref, tab, 0)
    halves_in_rows(got_ref, tab, 2 * cells)

    group_lo[...] = jnp.zeros_like(group_lo)
    group_hi[...] = jnp.zeros_like(group_hi)

    def features(ref, first, stage, is_target):
        def step(i, carry):
            at = pl.multiple_of(i * 8, 8)
            block = [ref[pl.ds(at * 4 + a, 8, stride=4), :] for a in range(4)]
            axes = [pieces(b - 0.5, 2) for b in block[:3]]
            norm = jnp.zeros((8, LANES), F32)
            for high, low in axes:
                norm = norm + (high + low) * (high + low)
            one = jnp.ones((8, LANES), F32)
            highs = [a[0] for a in axes]
            lows = [a[1] for a in axes]
            if is_target:
                twice = [-2.0 * h for h in highs], [-2.0 * v for v in lows]
                rows = twice[0] * 2 + twice[1] * 2 + pieces(norm, 3) + [one] * 3
            else:
                rows = (highs + lows) * 2 + [one] * 3 + pieces(norm + SOFTENING, 3)
                charge[pl.ds(first + at, 8), :] = block[3]
            for k, row in enumerate(rows):
                stage[pl.ds(at * FEAT + k, 8, stride=FEAT), :] = row
            return carry

        lax.fori_loop(0, ref.shape[0] // 32, step, 0, unroll=4)

    def packed(stage, out, first, count):
        def step(i, carry):
            out[first + i] = stage[pl.ds(pl.multiple_of(i * FEAT, FEAT), FEAT), :].astype(BF16)
            return carry

        lax.fori_loop(0, count, step, 0, unroll=8)

    rank_rows = coded_ref.shape[0] // scale_ref.shape[0]
    is_charge = charge_rows(rank_rows)

    def decode(r, carry):
        at = pl.ds(pl.multiple_of(r * rank_rows, rank_rows), rank_rows)
        code = coded_ref[at, :].astype(jnp.int32).astype(F32)
        unit = scale_ref[pl.ds(r, 1), :] * (1.0 / CHARGE_STEPS)
        place = (code + 32768.0) * (1.0 / PLACE_STEPS)
        gotp_ref[at, :] = jnp.where(is_charge, code * unit, place)
        return carry

    lax.fori_loop(0, scale_ref.shape[0], decode, 0, unroll=4)

    features(ownp_ref, 0, group_lo, True)
    packed(group_lo, target, 0, cells)
    features(ownp_ref, 0, group_hi, False)
    packed(group_hi, source, 0, cells)
    features(gotp_ref, cells, group_lo, False)
    packed(group_lo, source, cells, gotp_ref.shape[0] // 4)

    near_copy.wait()
    op_ids = lax.broadcasted_iota(jnp.int32, (op_count, list_pad), 0)

    def group(cell, buf):
        low = buf[pl.ds(0, list_pad, stride=2), :].astype(BF16)
        high = buf[pl.ds(1, list_pad, stride=2), :].astype(BF16)
        hot = jnp.where(op_ids == op_ref[pl.ds(cell, 1), :], 1.0, 0.0).astype(BF16)
        out = jnp.dot(hot, jnp.concatenate([low, high], 1), preferred_element_type=F32)
        group_lo[pl.ds(cell, op_count, stride=pitch), :] = out[:, :LANES]
        group_hi[pl.ds(cell, op_count, stride=pitch), :] = out[:, LANES:]

    def reduced(total, cell):
        pot_ref[pl.ds(cell, 1), :] = jnp.sum(total.T, axis=0, keepdims=True)

    per_pair = -(-list_width // ((near_count + 1) // 2))

    def leaves(c, carry):
        pending = None
        for u in range(UNROLL):
            cell = c * UNROLL + u
            x = target[cell]
            slot = u // WINDOW
            if u % WINDOW == 0:
                fetch(slot, 2 * c + slot).wait()
            src_at = (u % WINDOW) * list_width
            near_at = cell * near_count
            total = jnp.zeros((LANES, LANES), F32)
            taken = 0
            for p in range(0, near_count, 2):
                for j in range(taken, min(taken + per_pair, list_width)):
                    row = pl.multiple_of(windows[slot][src_at + j], 2)
                    picked[u][2 * j : 2 * j + 2, :] = tab[pl.ds(row, 2), :]
                taken += per_pair
                ids = [near_ref[near_at + n] for n in range(p, min(p + 2, near_count))]
                y = [source[i] for i in ids]
                y = jnp.concatenate(y, axis=1) if len(y) > 1 else y[0]
                dist = lax.dot_general(
                    x, y, (((0,), (0,)), ((), ())), preferred_element_type=F32
                )
                for t, i in enumerate(ids):
                    part = lax.rsqrt(dist[:, t * LANES : (t + 1) * LANES])
                    total = total + part * charge[pl.ds(i, 1), :]
                if p == 4:
                    group(jnp.maximum(cell - 1, 0), picked[(u - 1) % UNROLL])
                if p == 8 and pending is not None:
                    reduced(*pending)
            pending = (total, cell)
            if u % WINDOW == WINDOW - 1:

                @pl.when(c + 1 < cells // UNROLL)
                def _():
                    fetch(slot, 2 * (c + 1) + slot).start()

        reduced(*pending)
        return carry

    lax.fori_loop(0, cells // UNROLL, leaves, 0)
    group(cells - 1, picked[UNROLL - 1])

    for out, column in ((lower_ref, 0), (upper_ref, 1)):
        for s in range(MCAP):
            leaf = s if column == 0 else cells - 1 - s
            kept = s < moves_ref[0, column]
            block = ownp_ref[4 * leaf : 4 * leaf + 4, :]
            out[s, 0:4, :] = jnp.where(kept, block, 0.0)
            out[s, 4:5, :] = jnp.where(kept, pot_ref[leaf : leaf + 1, :], 0.0)

    tr_copy.wait()
    far = jnp.concatenate([far_ref[...]] * (cells // 8), 0)
    local_ref[...] = far
    width = 2 * LANES

    def translate(k, carry):
        parts = []
        for kk in range(KSTEP):
            at = pl.ds(pl.multiple_of((k * KSTEP + kk) * pitch, 8), cells)
            parts += [group_lo[at, :].astype(BF16), group_hi[at, :].astype(BF16)]
        ops = tr_ref[pl.ds(k * KSTEP, KSTEP)].reshape(KSTEP * width, width)
        local_ref[...] += jnp.dot(
            jnp.concatenate(parts, 1), ops, preferred_element_type=F32
        )
        return carry

    lax.fori_loop(0, op_count // KSTEP, translate, 0)


def main_call(
    list_width, src, near, ops, own, got, own_p, got_p, scale, far, moves, translate_ops
):
    cells = own.shape[0]
    list_pad = ops.shape[1]
    op_count = translate_ops.shape[0]
    tables = cells + got_p.shape[0] // 4
    pitch = cells + 8
    hbm = pl.BlockSpec(memory_space=pl.ANY)
    vmem = pl.BlockSpec(memory_space=pltpu.VMEM)
    return pl.pallas_call(
        functools.partial(
            main_kernel, list_width=list_width, op_count=op_count, pitch=pitch
        ),
        out_shape=(
            jax.ShapeDtypeStruct((cells, 2 * LANES), F32),
            jax.ShapeDtypeStruct((cells, LANES), F32),
            jax.ShapeDtypeStruct((MCAP, 5, LANES), F32),
            jax.ShapeDtypeStruct((MCAP, 5, LANES), F32),
        ),
        in_specs=[hbm, hbm] + [vmem] * 7 + [pl.BlockSpec(memory_space=pltpu.SMEM), hbm],
        out_specs=(vmem,) * 4,
        scratch_shapes=[
            pltpu.VMEM((2 * (cells + got.shape[0]), LANES), F32),
            pltpu.VMEM((tables, LANES), F32),
            pltpu.VMEM((cells, FEAT, LANES), BF16),
            pltpu.VMEM((tables, FEAT, LANES), BF16),
            pltpu.VMEM((op_count * pitch, LANES), F32),
            pltpu.VMEM((op_count * pitch, LANES), F32),
            pltpu.VMEM(translate_ops.shape, BF16),
            pltpu.SMEM((src.shape[0] * WINDOW // cells,), jnp.int32),
            pltpu.SMEM((src.shape[0] * WINDOW // cells,), jnp.int32),
            pltpu.SMEM(near.shape, jnp.int32),
            pltpu.SemaphoreType.DMA((4,)),
            pltpu.VMEM(got_p.shape, F32),
        ]
        + [pltpu.VMEM((2 * list_pad, LANES), F32)] * UNROLL,
        compiler_params=pltpu.CompilerParams(vmem_limit_bytes=60 * 1024 * 1024),
    )(src, near, ops, own, got, own_p, got_p, scale, far, moves, translate_ops)


def per_device(
    multipole,
    positions,
    charges,
    translate_ops,
    upward_ops,
    downward_ops,
    top_weight,
    send_cells,
    send_leaves,
    list_source,
    list_operator,
    near_leaves,
    move_counts,
):
    cells, width = multipole.shape
    leaf_size = positions.shape[2]
    ranks = lax.axis_size(AXES)

    body = jnp.concatenate([positions, charges[:, None, :]], 1)
    flat = body.reshape(-1, leaf_size)
    out_cells, out_body, share = pack(
        (send_cells * 2).reshape(-1),
        (send_leaves * 4).reshape(-1),
        multipole,
        flat,
        upward_ops,
        ranks,
    )
    got_cells, got_body, far, scale = exchange(
        top_weight.reshape(-1), share, downward_ops, out_cells, out_body
    )
    list_pad = -(-list_operator.shape[1] // 64) * 64
    ops = jnp.pad(
        list_operator,
        ((0, 0), (0, list_pad - list_operator.shape[1])),
        constant_values=translate_ops.shape[0],
    )
    flat_lists = (list_source * 2).reshape(cells // WINDOW, -1)
    span = -(-flat_lists.shape[1] // 1024) * 1024
    flat_lists = jnp.pad(flat_lists, ((0, 0), (0, span - flat_lists.shape[1])))
    local_exp, potential, lower, upper = main_call(
        list_source.shape[1],
        flat_lists.reshape(-1),
        near_leaves.reshape(-1),
        ops,
        multipole,
        got_cells.reshape(-1, width),
        flat,
        got_body.reshape(-1, leaf_size),
        scale,
        far,
        move_counts,
        translate_ops,
    )

    from_upper = shifted(lower, AXES, -1)
    from_lower = shifted(upper, AXES, 1)
    arrivals = jnp.concatenate([from_upper, from_lower], 0)
    return (local_exp, potential, arrivals)


def solution(mesh):
    rows = P(AXES, None)
    blocks = P(AXES, None, None)
    placed = (rows, blocks, rows) + (P(),) * 4 + (rows,) * 6
    return jax.shard_map(
        per_device,
        mesh=mesh,
        in_specs=placed,
        out_specs=(rows, rows, blocks),
        check_vma=False,
    )
```
